256 devices in a mesh: head: 4 (over y), seq: 64 (over x, z, core).
Axes of the slice: x: 4, y: 4, z: 8, core: 2. Of those that a mesh axis runs over, the one named last changes fastest.
Arguments:
- queries: bfloat16 [4, 8192], P(None, ('head', 'seq')), may hold values from -20 to 20
- key_cache: bfloat16 [4, 8, 65536, 128], P(None, 'head', 'seq'), may hold values from -16 to 16
- value_cache: bfloat16 [4, 8, 65536, 128], P(None, 'head', 'seq'), may hold values from -5 to 5
- page_list: int32 [4, 8, 256], P(None, 'head'), may hold values from 0 to 4095, as said below
- shard_counts: int32 [4, 8, 64], P(None, 'head'), may hold values from 0 to 8, as said below
- out_weight: bfloat16 [8192, 8192], P(('head', 'seq')), may hold values from -0.25 to 0.25
Outputs:
- output: bfloat16 [4, 8192], P(None, ('head', 'seq'))
- attention: bfloat16 [4, 8192], P(None, ('head', 'seq'))
- page_mass: float32 [4, 64, 4096], P(None, 'head', 'seq')
The draws below stay inside these ranges and needn't reach their ends.
Inputs may be any that keep to these rules, and one draw needn't show every extreme that they name: With live = the sum of shard_counts[b, g, :], entries 0 to live - 1 of page_list[b, g] are distinct pages in ascending order, and exactly shard_counts[b, g, s] of them lie in pages s * 64 to (s + 1) * 64 - 1; entries from live on are padding. `shard_counts`: exactly 8 for some index s of every batch row and KV head; the sum over s is at most 256.
All inputs are finite; a program needn't handle non-finite values.
Results may differ from the reference program's by a relative error of at most 0.0052.
Values may be sent and summed in bfloat16 or wider, within the bound.
No kernel may reach another device: no remote copies, remote signals or barrier semaphores. Data moves between devices by JAX's collectives and lax.ppermute only.
A program may use at most 64 MiB of HBM per device.

```python
import math
import jax
import jax.numpy as jnp
from jax import lax

D = 8192
HQ = 64
KVH = 8
HD = 128
PAGE = 16
BATCH = 4
CAP = 8
SELECT = 256
PAGES_DEV = 64
CONTEXT = 65536
NPAGES = 4096


def selection(key):
    shards = NPAGES // PAGES_DEV
    halves = shards // 2
    streams = jax.random.split(jax.random.fold_in(key, 7001), 6)
    leading = jax.random.randint(streams[0], (BATCH, KVH, halves), 0, CAP + 1)
    forced = jax.random.randint(streams[2], (BATCH, KVH, 1), 0, halves)
    leading = jnp.where(jnp.arange(halves)[None, None, :] == forced, CAP, leading)
    extra = jax.random.randint(streams[1], (BATCH, KVH, halves), 0, CAP + 1)
    trailing = extra % (CAP - leading + 1)
    raw_counts = jnp.concatenate([leading, trailing], axis=2)
    shuffle = jax.random.permutation(streams[3], jnp.broadcast_to(jnp.arange(shards), (BATCH, KVH, shards)), axis=2, independent=True)
    counts = jnp.take_along_axis(raw_counts, shuffle, axis=2).astype(jnp.int32)
    ranks = jax.random.permutation(streams[4], jnp.broadcast_to(jnp.arange(PAGES_DEV), (BATCH, KVH, shards, PAGES_DEV)), axis=3, independent=True)
    flags = (ranks < counts[..., None]).reshape(BATCH, KVH, NPAGES).astype(jnp.int32)
    running = jnp.cumsum(flags, axis=2)
    live_pages = running[:, :, -1]
    slot_ids = jnp.arange(SELECT)
    found = jnp.sum((running[:, :, None, :] <= slot_ids[None, None, :, None]).astype(jnp.int32), axis=3)
    filler = jax.random.randint(streams[5], (BATCH, KVH, SELECT), 0, NPAGES)
    pages = jnp.where(slot_ids[None, None, :] < live_pages[..., None], found, filler).astype(jnp.int32)
    return (counts, pages)


def draw_page_list(key, part):
    return selection(key)[1]


def draw_shard_counts(key, part):
    return selection(key)[0]


def draw_queries(key, part):
    group_size = HQ // KVH
    noise = jnp.clip(jax.random.normal(jax.random.fold_in(key, 11), (BATCH, KVH, group_size, HD), jnp.float32), -4.0, 4.0)
    sample = noise * 2.5
    return jnp.clip(sample, -20.0, 20.0).reshape(BATCH, HQ * HD).astype(jnp.bfloat16)


def draw_key_cache(key, part):
    noise = jnp.clip(jax.random.normal(jax.random.fold_in(key, 21), (BATCH, KVH, CONTEXT, HD), jnp.float32), -4.0, 4.0)
    sample = noise
    return jnp.clip(sample, -16.0, 16.0).astype(jnp.bfloat16)


def raised(array, own_key, source, target, shards_of, factor):
    def block_of(position):
        return (jnp.arange(array.shape[position]) // (array.shape[position] // shards_of)).reshape((-1,) + (1,) * (array.ndim - 1 - position))

    first = jax.random.permutation(own_key, shards_of)[block_of(target)]
    other_side = (block_of(target) + shards_of // 2) % shards_of
    return jnp.where((block_of(source) == first) | (block_of(source) == other_side), factor * array, array)


def block_scale(key, dims, cuts, least, largest):
    loudness = 1.0
    for position, blocks in cuts:
        draws = jax.random.uniform(jax.random.fold_in(jax.random.fold_in(key, 6), position), (blocks,), jnp.float32, least / len(cuts), largest / len(cuts))
        loudness = loudness * jnp.repeat(jnp.exp(draws), dims[position] // blocks).reshape((-1,) + (1,) * (len(dims) - 1 - position))
    return loudness


def normal_values(rng, extent, scale, most, cuts=(), kind=jnp.bfloat16):
    entries = jax.random.normal(rng, extent, jnp.float32) * scale
    if len(cuts) > 0:
        entries = block_scale(rng, extent, cuts, -0.22, 0.18) * entries
    return jnp.clip(entries, min=-most, max=most).astype(kind)


def gaussian_with(key, extent, width, reach, cuts, heavy, kind=jnp.bfloat16):
    drawn = width * jax.random.normal(key, extent, jnp.float32)
    if cuts:
        drawn = drawn * block_scale(key, extent, cuts, -0.22, 0.18)
    return jnp.clip(raised(drawn, jax.random.fold_in(key, 3), *heavy), -reach, reach).astype(kind)


def setup_inputs(seed: int = 0) -> dict:
    key_of = jax.random.split(jax.random.key(seed), 7)
    queries = draw_queries(jax.random.fold_in(key_of[6], 71), 0)
    key_cache = draw_key_cache(jax.random.fold_in(key_of[6], 71), 0)
    value_cache = normal_values(key_of[2], (BATCH, KVH, CONTEXT, HD), 1.0, 5.0, ((1, 4), (2, 64)))
    page_list = draw_page_list(jax.random.fold_in(key_of[6], 71), 0)
    shard_counts = draw_shard_counts(jax.random.fold_in(key_of[6], 71), 0)
    out_weight = gaussian_with(key_of[5], (HQ * HD, D), (HQ * HD) ** -0.5, 0.25, ((0, 256),), (0, 1, 256, 6.0))
    return dict(queries=queries, key_cache=key_cache, value_cache=value_cache, page_list=page_list, shard_counts=shard_counts, out_weight=out_weight)


def pick_pages(table, chosen):
    return table[chosen]

def reference(queries, key_cache, value_cache, page_list, shard_counts, out_weight):
    group_size = HQ // KVH
    score_scale = 1.0 / math.sqrt(HD)
    query_heads = queries.astype(jnp.float32).reshape(BATCH, KVH, group_size, HD)
    live_pages = lax.optimization_barrier(jnp.sum(shard_counts, axis=2))

    def per_head(head_index):
        query_group = lax.dynamic_index_in_dim(query_heads, head_index, 1, keepdims=False)
        head_keys = lax.dynamic_index_in_dim(key_cache, head_index, 1, keepdims=False)
        head_values = lax.dynamic_index_in_dim(value_cache, head_index, 1, keepdims=False)
        head_pages = lax.dynamic_index_in_dim(page_list, head_index, 1, keepdims=False)
        head_live = lax.dynamic_index_in_dim(live_pages, head_index, 1, keepdims=False)
        paged_keys = head_keys.astype(jnp.float32).reshape(BATCH, NPAGES, PAGE, HD)
        lower_keys = lax.optimization_barrier(jnp.min(paged_keys, axis=2))
        upper_keys = lax.optimization_barrier(jnp.max(paged_keys, axis=2))
        page_bound = lax.optimization_barrier(jnp.sum(jnp.maximum(query_group[:, :, None, :] * lower_keys[:, None, :, :], query_group[:, :, None, :] * upper_keys[:, None, :, :]), axis=3)) * score_scale
        page_peak = lax.optimization_barrier(jnp.max(page_bound, axis=2, keepdims=True))
        page_terms = jnp.exp(page_bound - page_peak)
        page_mass = page_terms / lax.optimization_barrier(jnp.sum(page_terms, axis=2, keepdims=True))
        paged_values = head_values.astype(jnp.float32).reshape(BATCH, NPAGES, PAGE, HD)
        chosen_keys = jax.vmap(pick_pages)(paged_keys, head_pages).reshape(BATCH, SELECT * PAGE, HD)
        chosen_values = jax.vmap(pick_pages)(paged_values, head_pages).reshape(BATCH, SELECT * PAGE, HD)
        scores = jnp.einsum('bjd,btd->bjt', query_group, chosen_keys, precision=lax.Precision.HIGHEST) * score_scale
        slot_live = (jnp.arange(SELECT * PAGE, dtype=jnp.int32) // PAGE)[None, :] < head_live[:, None]
        masked = jnp.where(slot_live[:, None, :], scores, -jnp.inf)
        global_top = lax.optimization_barrier(jnp.max(masked, axis=2, keepdims=True))
        weights = jnp.where(slot_live[:, None, :], jnp.exp(masked - global_top), 0.0)
        head_totals = lax.optimization_barrier(jnp.sum(weights, axis=2, keepdims=True))
        rounded = weights.astype(jnp.bfloat16).astype(jnp.float32)
        unnormed = jnp.einsum('bjt,btd->bjd', rounded, chosen_values, precision=lax.Precision.HIGHEST)
        attention = (unnormed / head_totals).astype(jnp.bfloat16)
        return (page_mass, attention)
    masses, attentions = lax.map(per_head, jnp.arange(KVH, dtype=jnp.int32))
    page_mass = jnp.transpose(masses, (1, 0, 2, 3)).reshape(BATCH, HQ, NPAGES)
    attention = jnp.transpose(attentions, (1, 0, 2, 3)).reshape(BATCH, HQ * HD)
    output = jnp.dot(attention, out_weight, preferred_element_type=jnp.float32).astype(jnp.bfloat16)
    return (output, attention, page_mass)
```

```python
import functools
import math

import jax
import jax.numpy as jnp
from jax import lax
from jax.experimental import pallas as pl
from jax.experimental.pallas import tpu as pltpu
from jax.sharding import PartitionSpec as P

HQ = 64
KVH = 8
HD = 128
PAGE = 16
CAP = 8
LANES = 128
NEGATIVE = -1e30
SCALE = 1.0 / math.sqrt(HD)

VMEM = pl.BlockSpec(memory_space=pltpu.VMEM)
SMEM = pl.BlockSpec(memory_space=pltpu.SMEM)


def block_lanes(shape, width):
    return lax.broadcasted_iota(jnp.int32, shape, 1) // width


def spread_kernel(copies, query_ref, out_ref):
    rows = query_ref[...].astype(jnp.float32)
    line = jnp.concatenate([rows[b : b + 1, :] for b in range(rows.shape[0])], axis=1)
    out_ref[...] = jnp.broadcast_to(line, (copies, LANES))


def prepare_kernel(counts_ref, pages_ref, key_ref, value_ref, ends_ref, keys_out, values_out):
    batch, groups, tokens, dim = key_ref.shape
    pages = tokens // PAGE
    shard = lax.axis_index("seq")
    pairs = [(b, g) for b in range(batch) for g in range(groups)]

    def before(s, sums):
        return tuple(t + counts_ref[b, g, s] for t, (b, g) in zip(sums, pairs))

    offsets = lax.fori_loop(0, shard, before, (jnp.int32(0),) * len(pairs))
    for n, (b, g) in enumerate(pairs):
        count = counts_ref[b, g, shard]
        for slot in range(CAP):
            at = jnp.minimum(offsets[n] + slot, pages_ref.shape[2] - 1)
            page = jnp.where(slot < count, pages_ref[b, g, at] - shard * pages, 0)
            page = jnp.clip(page, 0, pages - 1)
            start = pl.multiple_of(page * PAGE, PAGE)
            keys_out[n, slot * PAGE : (slot + 1) * PAGE, :] = key_ref[b, g, pl.ds(start, PAGE), :]
            values_out[n, slot * PAGE : (slot + 1) * PAGE, :] = value_ref[b, g, pl.ds(start, PAGE), :]
        paged = key_ref[b, g].reshape(pages, PAGE, dim)
        ends_ref[n, :, :dim] = jnp.max(paged, axis=1)
        ends_ref[n, :, dim:] = jnp.min(paged, axis=1)


def scores_kernel(counts_ref, query_ref, ends_ref, keys_ref, values_ref, part_ref, bound_ref):
    batch, groups, _ = counts_ref.shape
    heads = query_ref.shape[0] // 4
    group = heads // groups
    width = LANES // 4
    shard = lax.axis_index("seq")
    quarters = [query_ref[pl.ds(q, heads, stride=4), :] for q in range(4)]
    lane_block = block_lanes((heads, LANES), width)

    def rows_of(b):
        found = jnp.zeros((heads, LANES), jnp.float32)
        for q in range(4):
            shift = (q - b) * width % LANES
            moved = pltpu.roll(quarters[q], shift, 1) if shift else quarters[q]
            found = jnp.where(lane_block == q, moved, found)
        return found

    lanes = lax.broadcasted_iota(jnp.int32, (group, LANES), 1)
    subs = lax.broadcasted_iota(jnp.int32, (group, LANES), 0)
    page_row = jnp.zeros((group, LANES), jnp.float32)
    head_rows = [jnp.zeros((group, LANES), jnp.float32) for _ in range(groups)]
    mixed = []
    contract = (((1,), (1,)), ((), ()))
    for b in range(batch):
        rows = rows_of(b)
        parts = []
        for g in range(groups):
            n = b * groups + g
            query = rows[g * group : (g + 1) * group]
            signed = jnp.concatenate([jnp.maximum(query, 0.0), jnp.minimum(query, 0.0)], axis=1)
            bound = SCALE * lax.dot_general(
                signed.astype(jnp.bfloat16), ends_ref[n], contract, preferred_element_type=jnp.float32
            )
            bound_ref[b, g * group : (g + 1) * group, :] = bound
            peak = jnp.max(bound, axis=1, keepdims=True)
            mass = jnp.sum(jnp.exp(bound - peak), axis=1, keepdims=True)
            page_row = jnp.where(lanes == subs * (batch * groups) + n, peak + jnp.log(mass), page_row)
            scores = SCALE * lax.dot_general(
                query.astype(jnp.bfloat16), keys_ref[n], contract, preferred_element_type=jnp.float32
            )
            live = lanes // PAGE < counts_ref[b, g, shard]
            scores = jnp.where(live, scores, NEGATIVE)
            top = jnp.max(scores, axis=1, keepdims=True)
            weights = jnp.where(live, jnp.exp(scores - top), 0.0)
            total = jnp.maximum(jnp.sum(weights, axis=1, keepdims=True), 1e-30)
            unnormed = jnp.dot(
                weights.astype(jnp.bfloat16), values_ref[n], preferred_element_type=jnp.float32
            )
            parts.append(unnormed / total)
            head_rows[g] = jnp.where(
                lanes == LANES // 2 + b, top + jnp.log(total), head_rows[g]
            )
        mixed.append(jnp.concatenate(parts, axis=0))
    page_line = jnp.sum(page_row, axis=0, keepdims=True)
    seconds = jnp.concatenate(head_rows, axis=0) + page_line
    for q in range(4):
        line = jnp.zeros((heads, LANES), jnp.float32)
        for b in range(batch):
            shift = (b - q) * width % LANES
            moved = pltpu.roll(mixed[b], shift, 1) if shift else mixed[b]
            line = jnp.where(lane_block == b, moved, line)
        part_ref[pl.ds(2 * q, heads, stride=8), :] = line
        part_ref[pl.ds(2 * q + 1, heads, stride=8), :] = seconds


def project_kernel(part_ref, weight_ref, attention_ref, out_ref):
    shards = part_ref.shape[0] // 2
    width = LANES // 4
    values = part_ref[pl.ds(0, shards, stride=2), :]
    logs = part_ref[pl.ds(1, shards, stride=2), :]
    shares = jnp.exp(logs - jnp.max(logs, axis=0, keepdims=True))
    block = block_lanes((shards, LANES), width)
    spread = jnp.zeros((shards, LANES), jnp.float32)
    for b in range(4):
        at = LANES // 2 + b
        spread = jnp.where(block == b, shares[:, at : at + 1], spread)
    line = jnp.sum(spread * values, axis=0, keepdims=True) / jnp.sum(spread, axis=0, keepdims=True)
    for b in range(4):
        attention_ref[b : b + 1, :] = line[:, b * width : (b + 1) * width].astype(jnp.bfloat16)
    line = line.astype(jnp.bfloat16).astype(jnp.float32)
    lanes = lax.broadcasted_iota(jnp.int32, (width, LANES), 1)
    subs = lax.broadcasted_iota(jnp.int32, (width, LANES), 0)
    picked = jnp.where(lanes % width == subs, line, 0.0).astype(jnp.bfloat16)
    same = (
        lax.broadcasted_iota(jnp.int32, (LANES, LANES), 0) // width
        == block_lanes((LANES, LANES), width)
    )
    turned = jnp.dot(
        picked, jnp.where(same, 1.0, 0.0).astype(jnp.bfloat16), preferred_element_type=jnp.float32
    )
    diagonal = lanes % width == subs
    wide = jnp.concatenate(
        [jnp.where(diagonal, turned[k : k + 1, :], 0.0).astype(jnp.bfloat16) for k in range(width)],
        axis=0,
    )
    out_ref[...] = jnp.dot(weight_ref[...], wide, preferred_element_type=jnp.float32)


def mass_kernel(part_ref, bound_ref, mass_ref):
    batch, heads, pages = bound_ref.shape
    shards = part_ref.shape[0] // 2
    group = HQ // KVH
    groups = heads // group
    logs = part_ref[pl.ds(1, shards, stride=2), :]
    peak = jnp.max(logs, axis=0, keepdims=True)
    line = peak + jnp.log(jnp.sum(jnp.exp(logs - peak), axis=0, keepdims=True))
    lanes = lax.broadcasted_iota(jnp.int32, (group, LANES), 1)
    subs = lax.broadcasted_iota(jnp.int32, (group, LANES), 0)
    for b in range(batch):
        for g in range(groups):
            n = b * groups + g
            column = jnp.sum(
                jnp.where(lanes == subs * (batch * groups) + n, line, 0.0), axis=1, keepdims=True
            )
            rows = slice(g * group, (g + 1) * group)
            mass_ref[b, rows, :] = jnp.exp(bound_ref[b, rows, :] - column)


def total_kernel(width, terms_ref, out_ref):
    line = jnp.sum(terms_ref[...], axis=0, keepdims=True)
    for b in range(out_ref.shape[0]):
        out_ref[b : b + 1, :] = line[:, b * width : (b + 1) * width].astype(out_ref.dtype)


def call(kernel, out_shape, args, specs, nbytes, flops=0):
    many = isinstance(out_shape, tuple)
    return pl.pallas_call(
        kernel,
        out_shape=out_shape,
        in_specs=specs,
        out_specs=tuple(VMEM for _ in out_shape) if many else VMEM,
        compiler_params=pltpu.CompilerParams(vmem_limit_bytes=32 * 1024 * 1024),
        cost_estimate=pl.CostEstimate(flops=flops, bytes_accessed=nbytes, transcendentals=0),
    )(*args)


def exchanged(x, axis):
    rows = lax.axis_size(axis)
    sent = x.reshape(rows, x.shape[0] // rows, x.shape[1])
    return lax.all_to_all(sent, axis, 0, 0, tiled=True).reshape(x.shape)


def local(queries, key_cache, value_cache, page_list, shard_counts, out_weight):
    batch, groups, tokens, dim = key_cache.shape
    pages = tokens // PAGE
    shards = lax.axis_size("seq")
    devices = lax.axis_size("head") * shards
    pairs = batch * groups
    heads = groups * (HQ // KVH)
    width = queries.shape[1]
    f32, bf16 = jnp.float32, jnp.bfloat16
    S = jax.ShapeDtypeStruct

    sent = call(functools.partial(spread_kernel, shards), S((shards, LANES), f32), (queries,), [VMEM], 1 << 16)
    ends, keys, values = call(
        prepare_kernel,
        (S((pairs, pages, 2 * dim), bf16), S((pairs, CAP * PAGE, dim), bf16), S((pairs, CAP * PAGE, dim), bf16)),
        (shard_counts, page_list, key_cache, value_cache),
        [SMEM, SMEM, VMEM, VMEM],
        1 << 23,
    )
    gathered = exchanged(sent, "seq")
    weight = jnp.transpose(out_weight.reshape(width, devices, width), (1, 0, 2)).reshape(devices, width * width)
    parts, bound = call(
        scores_kernel,
        (S((2 * shards, LANES), f32), S((batch, heads, pages), f32)),
        (shard_counts, gathered, ends, keys, values),
        [SMEM, VMEM, VMEM, VMEM, VMEM],
        1 << 20,
    )
    arrived = exchanged(parts, "seq")
    attention, terms = call(
        project_kernel,
        (S((batch, width), bf16), S((devices, LANES), f32)),
        (arrived, weight),
        [VMEM, VMEM],
        1 << 20,
    )
    page_mass = call(mass_kernel, S((batch, heads, pages), f32), (arrived, bound), [VMEM, VMEM], 1 << 18)
    landed = exchanged(terms, ("head", "seq"))
    output = call(functools.partial(total_kernel, width), S((batch, width), bf16), (landed,), [VMEM], 1 << 17)
    return (output, attention, page_mass)


def solution(mesh):
    return jax.shard_map(
        local,
        mesh=mesh,
        in_specs=(
            P(None, ("head", "seq")),
            P(None, "head", "seq", None),
            P(None, "head", "seq", None),
            P(None, "head", None),
            P(None, "head", None),
            P(("head", "seq"), None),
        ),
        out_specs=(P(None, ("head", "seq")), P(None, ("head", "seq")), P(None, "head", "seq")),
        check_vma=False,
    )
```

```python
import functools
import math

import jax
import jax.numpy as jnp
from jax import lax
from jax.experimental import pallas as pl
from jax.experimental.pallas import tpu as pltpu
from jax.sharding import PartitionSpec as P

HQ = 64
KVH = 8
HD = 128
PAGE = 16
CAP = 8
LANES = 128
NEGATIVE = -1e30
SCALE = 1.0 / math.sqrt(HD)

VMEM = pl.BlockSpec(memory_space=pltpu.VMEM)
HBM = pl.BlockSpec(memory_space=pltpu.HBM)


def block_lanes(shape, width):
    return lax.broadcasted_iota(jnp.int32, shape, 1) // width


def spread_kernel(copies, query_ref, out_ref):
    rows = query_ref[...].astype(jnp.float32)
    line = jnp.concatenate([rows[b : b + 1, :] for b in range(rows.shape[0])], axis=1)
    out_ref[...] = jnp.broadcast_to(line, (copies, LANES))


def prepare_kernel(
    counts_hbm, pages_hbm, key_hbm, value_hbm,
    live_ref, ends_ref, keys_out, values_out,
    counts_ref, pages_ref, key_ref, value_ref, list_sems, key_sems, value_sems,
):
    batch, groups, tokens, dim = key_hbm.shape
    pages = tokens // PAGE
    shard = lax.axis_index("seq")
    pairs = [(b, g) for b in range(batch) for g in range(groups)]
    lists = [
        pltpu.make_async_copy(counts_hbm, counts_ref, list_sems.at[0]),
        pltpu.make_async_copy(pages_hbm, pages_ref, list_sems.at[1]),
    ]
    key_copies = [
        pltpu.make_async_copy(key_hbm.at[b, g], key_ref.at[n], key_sems.at[n])
        for n, (b, g) in enumerate(pairs)
    ]
    value_copies = [
        pltpu.make_async_copy(value_hbm.at[b, g], value_ref.at[n], value_sems.at[n])
        for n, (b, g) in enumerate(pairs)
    ]
    for copy in lists + key_copies + value_copies:
        copy.start()
    for copy in lists:
        copy.wait()
    chosen = []
    for n, (b, g) in enumerate(pairs):
        counts = counts_ref[b, g : g + 1, :]
        slots = lax.broadcasted_iota(jnp.int32, counts.shape, 1)
        offset = jnp.sum(jnp.where(slots < shard, counts, 0))
        count = jnp.sum(jnp.where(slots == shard, counts, 0), axis=1, keepdims=True)
        lanes = lax.broadcasted_iota(jnp.int32, (1, LANES), 1)
        live_ref[n : n + 1, :] = jnp.where(lanes // PAGE < count, 1.0, 0.0)
        starts = []
        for slot in range(CAP):
            at = jnp.minimum(offset + slot, pages_ref.shape[2] - 1)
            page = jnp.clip(pages_ref[b, g, at] - shard * pages, 0, pages - 1)
            starts.append(pl.multiple_of(page * PAGE, PAGE))
        chosen.append(starts)
    for n in range(len(pairs)):
        key_copies[n].wait()
        paged = key_ref[n].reshape(pages, PAGE, dim)
        ends_ref[n, :, :dim] = jnp.max(paged, axis=1)
        ends_ref[n, :, dim:] = jnp.min(paged, axis=1)
        for slot in range(CAP):
            keys_out[n, slot * PAGE : (slot + 1) * PAGE, :] = key_ref[n, pl.ds(chosen[n][slot], PAGE), :]
    for n in range(len(pairs)):
        value_copies[n].wait()
        for slot in range(CAP):
            values_out[n, slot * PAGE : (slot + 1) * PAGE, :] = value_ref[n, pl.ds(chosen[n][slot], PAGE), :]


def scores_kernel(live_ref, query_ref, ends_ref, keys_ref, values_ref, part_ref, bound_ref):
    batch, heads, _ = bound_ref.shape
    groups = live_ref.shape[0] // batch
    group = heads // groups
    width = LANES // 4
    quarters = [query_ref[pl.ds(q, heads, stride=4), :] for q in range(4)]
    lane_block = block_lanes((heads, LANES), width)

    def rows_of(b):
        found = jnp.zeros((heads, LANES), jnp.float32)
        for q in range(4):
            shift = (q - b) * width % LANES
            moved = pltpu.roll(quarters[q], shift, 1) if shift else quarters[q]
            found = jnp.where(lane_block == q, moved, found)
        return found

    lanes = lax.broadcasted_iota(jnp.int32, (group, LANES), 1)
    subs = lax.broadcasted_iota(jnp.int32, (group, LANES), 0)
    page_row = jnp.zeros((group, LANES), jnp.float32)
    head_rows = [jnp.zeros((group, LANES), jnp.float32) for _ in range(groups)]
    mixed = []
    contract = (((1,), (1,)), ((), ()))
    for b in range(batch):
        rows = rows_of(b)
        parts = []
        for g in range(groups):
            n = b * groups + g
            query = rows[g * group : (g + 1) * group]
            signed = jnp.concatenate([jnp.maximum(query, 0.0), jnp.minimum(query, 0.0)], axis=1)
            bound = SCALE * lax.dot_general(
                signed.astype(jnp.bfloat16), ends_ref[n], contract, preferred_element_type=jnp.float32
            )
            bound_ref[b, g * group : (g + 1) * group, :] = bound
            peak = jnp.max(bound, axis=1, keepdims=True)
            mass = jnp.sum(jnp.exp(bound - peak), axis=1, keepdims=True)
            page_row = jnp.where(lanes == subs * (batch * groups) + n, peak + jnp.log(mass), page_row)
            scores = SCALE * lax.dot_general(
                query.astype(jnp.bfloat16), keys_ref[n], contract, preferred_element_type=jnp.float32
            )
            live = live_ref[n : n + 1, :] > 0.0
            scores = jnp.where(live, scores, NEGATIVE)
            top = jnp.max(scores, axis=1, keepdims=True)
            weights = jnp.where(live, jnp.exp(scores - top), 0.0)
            total = jnp.maximum(jnp.sum(weights, axis=1, keepdims=True), 1e-30)
            unnormed = jnp.dot(
                weights.astype(jnp.bfloat16), values_ref[n], preferred_element_type=jnp.float32
            )
            parts.append(unnormed / total)
            head_rows[g] = jnp.where(
                lanes == LANES // 2 + b, top + jnp.log(total), head_rows[g]
            )
        mixed.append(jnp.concatenate(parts, axis=0))
    page_line = jnp.sum(page_row, axis=0, keepdims=True)
    seconds = jnp.concatenate(head_rows, axis=0) + page_line
    for q in range(4):
        line = jnp.zeros((heads, LANES), jnp.float32)
        for b in range(batch):
            shift = (b - q) * width % LANES
            moved = pltpu.roll(mixed[b], shift, 1) if shift else mixed[b]
            line = jnp.where(lane_block == b, moved, line)
        part_ref[pl.ds(2 * q, heads, stride=8), :] = line
        part_ref[pl.ds(2 * q + 1, heads, stride=8), :] = seconds


def project_kernel(part_ref, weight_ref, attention_ref, out_ref):
    shards = part_ref.shape[0] // 2
    width = LANES // 4
    values = part_ref[pl.ds(0, shards, stride=2), :]
    logs = part_ref[pl.ds(1, shards, stride=2), :]
    shares = jnp.exp(logs - jnp.max(logs, axis=0, keepdims=True))
    block = block_lanes((shards, LANES), width)
    spread = jnp.zeros((shards, LANES), jnp.float32)
    for b in range(4):
        at = LANES // 2 + b
        spread = jnp.where(block == b, shares[:, at : at + 1], spread)
    line = jnp.sum(spread * values, axis=0, keepdims=True) / jnp.sum(spread, axis=0, keepdims=True)
    for b in range(4):
        attention_ref[b : b + 1, :] = line[:, b * width : (b + 1) * width].astype(jnp.bfloat16)
    line = line.astype(jnp.bfloat16).astype(jnp.float32)
    lanes = lax.broadcasted_iota(jnp.int32, (width, LANES), 1)
    subs = lax.broadcasted_iota(jnp.int32, (width, LANES), 0)
    picked = jnp.where(lanes % width == subs, line, 0.0).astype(jnp.bfloat16)
    same = (
        lax.broadcasted_iota(jnp.int32, (LANES, LANES), 0) // width
        == block_lanes((LANES, LANES), width)
    )
    turned = jnp.dot(
        picked, jnp.where(same, 1.0, 0.0).astype(jnp.bfloat16), preferred_element_type=jnp.float32
    )
    diagonal = lanes % width == subs
    wide = jnp.concatenate(
        [jnp.where(diagonal, turned[k : k + 1, :], 0.0).astype(jnp.bfloat16) for k in range(width)],
        axis=0,
    )
    out_ref[...] = jnp.dot(weight_ref[...], wide, preferred_element_type=jnp.float32)


def mass_kernel(part_ref, bound_ref, mass_ref):
    batch, heads, pages = bound_ref.shape
    shards = part_ref.shape[0] // 2
    group = HQ // KVH
    groups = heads // group
    logs = part_ref[pl.ds(1, shards, stride=2), :]
    peak = jnp.max(logs, axis=0, keepdims=True)
    line = peak + jnp.log(jnp.sum(jnp.exp(logs - peak), axis=0, keepdims=True))
    lanes = lax.broadcasted_iota(jnp.int32, (group, LANES), 1)
    subs = lax.broadcasted_iota(jnp.int32, (group, LANES), 0)
    for b in range(batch):
        for g in range(groups):
            n = b * groups + g
            column = jnp.sum(
                jnp.where(lanes == subs * (batch * groups) + n, line, 0.0), axis=1, keepdims=True
            )
            rows = slice(g * group, (g + 1) * group)
            mass_ref[b, rows, :] = jnp.exp(bound_ref[b, rows, :] - column)


def total_kernel(width, terms_ref, out_ref):
    line = jnp.sum(terms_ref[...], axis=0, keepdims=True)
    for b in range(out_ref.shape[0]):
        out_ref[b : b + 1, :] = line[:, b * width : (b + 1) * width].astype(out_ref.dtype)


def call(kernel, out_shape, args, specs, nbytes, scratch=(), limit=32):
    many = isinstance(out_shape, tuple)
    return pl.pallas_call(
        kernel,
        out_shape=out_shape,
        in_specs=specs,
        out_specs=tuple(VMEM for _ in out_shape) if many else VMEM,
        scratch_shapes=list(scratch),
        compiler_params=pltpu.CompilerParams(vmem_limit_bytes=limit << 20),
        cost_estimate=pl.CostEstimate(flops=0, bytes_accessed=nbytes, transcendentals=0),
    )(*args)


def exchanged(x, axis):
    rows = lax.axis_size(axis)
    sent = x.reshape(rows, x.shape[0] // rows, x.shape[1])
    return lax.all_to_all(sent, axis, 0, 0, tiled=True).reshape(x.shape)


def local(queries, key_cache, value_cache, page_list, shard_counts, out_weight):
    batch, groups, tokens, dim = key_cache.shape
    pages = tokens // PAGE
    shards = lax.axis_size("seq")
    devices = lax.axis_size("head") * shards
    pairs = batch * groups
    heads = groups * (HQ // KVH)
    width = queries.shape[1]
    f32, bf16 = jnp.float32, jnp.bfloat16
    S = jax.ShapeDtypeStruct

    sent = call(
        functools.partial(spread_kernel, shards),
        S((shards, LANES), f32),
        (queries,),
        [VMEM],
        1 << 16,
    )
    live, ends, keys, values = call(
        prepare_kernel,
        (
            S((pairs, LANES), f32),
            S((pairs, pages, 2 * dim), bf16),
            S((pairs, CAP * PAGE, dim), bf16),
            S((pairs, CAP * PAGE, dim), bf16),
        ),
        (shard_counts, page_list, key_cache, value_cache),
        [HBM, HBM, HBM, HBM],
        1 << 23,
        [
            pltpu.VMEM(shard_counts.shape, jnp.int32),
            pltpu.SMEM(page_list.shape, jnp.int32),
            pltpu.VMEM((pairs, tokens, dim), bf16),
            pltpu.VMEM((pairs, tokens, dim), bf16),
            pltpu.SemaphoreType.DMA((2,)),
            pltpu.SemaphoreType.DMA((pairs,)),
            pltpu.SemaphoreType.DMA((pairs,)),
        ],
        53,
    )
    gathered = exchanged(sent, "seq")
    weight = jnp.transpose(out_weight.reshape(width, devices, width), (1, 0, 2)).reshape(devices, width * width)
    parts, bound = call(
        scores_kernel,
        (S((2 * shards, LANES), f32), S((batch, heads, pages), f32)),
        (live, gathered, ends, keys, values),
        [VMEM, VMEM, VMEM, VMEM, VMEM],
        1 << 20,
    )
    arrived = exchanged(parts, "seq")
    attention, terms = call(
        project_kernel,
        (S((batch, width), bf16), S((devices, LANES), f32)),
        (arrived, weight),
        [VMEM, VMEM],
        1 << 20,
    )
    page_mass = call(mass_kernel, S((batch, heads, pages), f32), (arrived, bound), [VMEM, VMEM], 1 << 18)
    landed = exchanged(terms, ("head", "seq"))
    output = call(functools.partial(total_kernel, width), S((batch, width), bf16), (landed,), [VMEM], 1 << 17)
    return (output, attention, page_mass)


def solution(mesh):
    return jax.shard_map(
        local,
        mesh=mesh,
        in_specs=(
            P(None, ("head", "seq")),
            P(None, "head", "seq", None),
            P(None, "head", "seq", None),
            P(None, "head", None),
            P(None, "head", None),
            P(("head", "seq"), None),
        ),
        out_specs=(P(None, ("head", "seq")), P(None, ("head", "seq")), P(None, "head", "seq")),
        check_vma=False,
    )
```

```python
import functools
import math

import jax
import jax.numpy as jnp
from jax import lax
from jax.experimental import pallas as pl
from jax.experimental.pallas import tpu as pltpu
from jax.sharding import PartitionSpec as P

HQ = 64
KVH = 8
HD = 128
PAGE = 16
CAP = 8
LANES = 128
NEGATIVE = -1e30
SCALE = 1.0 / math.sqrt(HD)

VMEM = pl.BlockSpec(memory_space=pltpu.VMEM)
HBM = pl.BlockSpec(memory_space=pltpu.HBM)


def block_lanes(shape, width):
    return lax.broadcasted_iota(jnp.int32, shape, 1) // width


def spread_kernel(copies, query_ref, out_ref):
    rows = query_ref[...].astype(jnp.float32)
    line = jnp.concatenate([rows[b : b + 1, :] for b in range(rows.shape[0])], axis=1)
    out_ref[...] = jnp.broadcast_to(line, (copies, LANES))


def prepare_kernel(
    counts_hbm, pages_hbm, key_hbm, value_hbm,
    live_ref, ends_ref, keys_out, values_out,
    counts_ref, pages_ref, key_ref, value_ref, list_sems, key_sems, value_sems,
):
    batch, groups, tokens, dim = key_hbm.shape
    pages = tokens // PAGE
    shard = lax.axis_index("seq")
    pairs = [(b, g) for b in range(batch) for g in range(groups)]
    lists = [
        pltpu.make_async_copy(counts_hbm, counts_ref, list_sems.at[0]),
        pltpu.make_async_copy(pages_hbm, pages_ref, list_sems.at[1]),
    ]
    key_copies = [
        pltpu.make_async_copy(key_hbm.at[b, g], key_ref.at[n], key_sems.at[n])
        for n, (b, g) in enumerate(pairs)
    ]
    value_copies = [
        pltpu.make_async_copy(value_hbm.at[b, g], value_ref.at[n], value_sems.at[n])
        for n, (b, g) in enumerate(pairs)
    ]
    for copy in lists + key_copies + value_copies:
        copy.start()
    for copy in lists:
        copy.wait()
    chosen = []
    for n, (b, g) in enumerate(pairs):
        counts = counts_ref[b, g : g + 1, :]
        slots = lax.broadcasted_iota(jnp.int32, counts.shape, 1)
        offset = jnp.sum(jnp.where(slots < shard, counts, 0))
        count = jnp.sum(jnp.where(slots == shard, counts, 0), axis=1, keepdims=True)
        lanes = lax.broadcasted_iota(jnp.int32, (1, LANES), 1)
        live_ref[n : n + 1, :] = jnp.where(lanes // PAGE < count, 1.0, 0.0)
        starts = []
        for slot in range(CAP):
            at = jnp.minimum(offset + slot, pages_ref.shape[2] - 1)
            page = jnp.clip(pages_ref[b, g, at] - shard * pages, 0, pages - 1)
            starts.append(pl.multiple_of(page * PAGE, PAGE))
        chosen.append(starts)
    for n in range(len(pairs)):
        key_copies[n].wait()
        paged = key_ref[n].reshape(pages, PAGE, dim)
        ends_ref[n, :, :dim] = jnp.max(paged, axis=1)
        ends_ref[n, :, dim:] = jnp.min(paged, axis=1)
        for slot in range(CAP):
            keys_out[n, slot * PAGE : (slot + 1) * PAGE, :] = key_ref[n, pl.ds(chosen[n][slot], PAGE), :]
    for n in range(len(pairs)):
        value_copies[n].wait()
        for slot in range(CAP):
            values_out[n, slot * PAGE : (slot + 1) * PAGE, :] = value_ref[n, pl.ds(chosen[n][slot], PAGE), :]


def scores_kernel(live_ref, query_ref, ends_ref, keys_ref, values_ref, part_ref, bound_ref):
    batch, heads, _ = bound_ref.shape
    groups = live_ref.shape[0] // batch
    group = heads // groups
    width = LANES // 4
    quarters = [query_ref[pl.ds(q, heads, stride=4), :] for q in range(4)]
    lane_block = block_lanes((heads, LANES), width)

    def rows_of(b):
        found = jnp.zeros((heads, LANES), jnp.float32)
        for q in range(4):
            shift = (q - b) * width % LANES
            moved = pltpu.roll(quarters[q], shift, 1) if shift else quarters[q]
            found = jnp.where(lane_block == q, moved, found)
        return found

    lanes = lax.broadcasted_iota(jnp.int32, (group, LANES), 1)
    subs = lax.broadcasted_iota(jnp.int32, (group, LANES), 0)
    page_row = jnp.zeros((group, LANES), jnp.float32)
    head_rows = [jnp.zeros((group, LANES), jnp.float32) for _ in range(groups)]
    mixed = []
    contract = (((1,), (1,)), ((), ()))
    for b in range(batch):
        rows = rows_of(b)
        parts = []
        for g in range(groups):
            n = b * groups + g
            query = rows[g * group : (g + 1) * group]
            signed = jnp.concatenate([jnp.maximum(query, 0.0), jnp.minimum(query, 0.0)], axis=1)
            bound = SCALE * lax.dot_general(
                signed.astype(jnp.bfloat16), ends_ref[n], contract, preferred_element_type=jnp.float32
            )
            bound_ref[b, g * group : (g + 1) * group, :] = bound
            peak = jnp.max(bound, axis=1, keepdims=True)
            mass = jnp.sum(jnp.exp(bound - peak), axis=1, keepdims=True)
            page_row = jnp.where(lanes == subs * (batch * groups) + n, peak + jnp.log(mass), page_row)
            scores = SCALE * lax.dot_general(
                query.astype(jnp.bfloat16), keys_ref[n], contract, preferred_element_type=jnp.float32
            )
            live = live_ref[n : n + 1, :] > 0.0
            scores = jnp.where(live, scores, NEGATIVE)
            top = jnp.max(scores, axis=1, keepdims=True)
            weights = jnp.where(live, jnp.exp(scores - top), 0.0)
            total = jnp.maximum(jnp.sum(weights, axis=1, keepdims=True), 1e-30)
            unnormed = jnp.dot(
                weights.astype(jnp.bfloat16), values_ref[n], preferred_element_type=jnp.float32
            )
            parts.append(unnormed / total)
            head_rows[g] = jnp.where(
                lanes == LANES // 2 + b, top + jnp.log(total), head_rows[g]
            )
        mixed.append(jnp.concatenate(parts, axis=0))
    page_line = jnp.sum(page_row, axis=0, keepdims=True)
    seconds = jnp.concatenate(head_rows, axis=0) + page_line
    for q in range(4):
        line = jnp.zeros((heads, LANES), jnp.float32)
        for b in range(batch):
            shift = (b - q) * width % LANES
            moved = pltpu.roll(mixed[b], shift, 1) if shift else mixed[b]
            line = jnp.where(lane_block == b, moved, line)
        part_ref[pl.ds(2 * q, heads, stride=8), :] = line
        part_ref[pl.ds(2 * q + 1, heads, stride=8), :] = seconds


def merged_line(part_ref):
    shards = part_ref.shape[0] // 2
    values = part_ref[pl.ds(0, shards, stride=2), :]
    logs = part_ref[pl.ds(1, shards, stride=2), :]
    shares = jnp.exp(logs - jnp.max(logs, axis=0, keepdims=True))
    block = block_lanes((shards, LANES), LANES // 4)
    spread = jnp.zeros((shards, LANES), jnp.float32)
    for b in range(4):
        at = LANES // 2 + b
        spread = jnp.where(block == b, shares[:, at : at + 1], spread)
    line = jnp.sum(spread * values, axis=0, keepdims=True) / jnp.sum(spread, axis=0, keepdims=True)
    return line.astype(jnp.bfloat16)


def project_kernel(part_ref, weight_ref, out_ref):
    width = LANES // 4
    columns = weight_ref.shape[1]
    chunk = 4 * LANES
    line = merged_line(part_ref).astype(jnp.float32)
    rows = [line[:, b * width : (b + 1) * width] for b in range(4)]
    small = lax.broadcasted_iota(jnp.int32, (8, width), 0)
    sides = []
    for d in range(4):
        side = jnp.zeros((8, width), jnp.float32)
        for b in range(4):
            side = jnp.where((small + d) % 4 == b, rows[b], side)
        sides.append(side)
    left = jnp.concatenate(sides, axis=0).astype(jnp.bfloat16)
    subs = lax.broadcasted_iota(jnp.int32, (8, LANES), 0)
    block = block_lanes((8, LANES), width)
    for start in range(0, columns, chunk):
        terms = jnp.dot(left, weight_ref[:, start : start + chunk], preferred_element_type=jnp.float32)
        for pair in range(0, chunk, 2 * LANES):
            found = jnp.zeros((8, LANES), jnp.float32)
            for d in range(4):
                turn = terms[8 * d : 8 * (d + 1), pair : pair + 2 * LANES]
                turn = jnp.where(subs < 4, turn[:, :LANES], turn[:, LANES:])
                turn = pltpu.roll(turn, d * width, 1) if d else turn
                found = jnp.where(block == (subs + d) % 4, turn, found)
            at = (start + pair) // width
            out_ref[at : at + 8, :] = found


def finish_kernel(terms_ref, part_ref, bound_ref, output_ref, attention_ref, mass_ref):
    batch, heads, pages = bound_ref.shape
    shards = part_ref.shape[0] // 2
    group = HQ // KVH
    groups = heads // group
    width = LANES // 4
    sums = jnp.sum(terms_ref[...], axis=0, keepdims=True)
    attention = merged_line(part_ref)
    for b in range(batch):
        columns = slice(b * width, (b + 1) * width)
        output_ref[b : b + 1, :] = sums[:, columns].astype(jnp.bfloat16)
        attention_ref[b : b + 1, :] = attention[:, columns]
    logs = part_ref[pl.ds(1, shards, stride=2), :]
    peak = jnp.max(logs, axis=0, keepdims=True)
    line = peak + jnp.log(jnp.sum(jnp.exp(logs - peak), axis=0, keepdims=True))
    lanes = lax.broadcasted_iota(jnp.int32, (group, LANES), 1)
    subs = lax.broadcasted_iota(jnp.int32, (group, LANES), 0)
    for b in range(batch):
        for g in range(groups):
            n = b * groups + g
            column = jnp.sum(
                jnp.where(lanes == subs * (batch * groups) + n, line, 0.0), axis=1, keepdims=True
            )
            rows = slice(g * group, (g + 1) * group)
            mass_ref[b, rows, :] = jnp.exp(bound_ref[b, rows, :] - column)


def call(kernel, out_shape, args, specs, nbytes, scratch=(), limit=32):
    many = isinstance(out_shape, tuple)
    return pl.pallas_call(
        kernel,
        out_shape=out_shape,
        in_specs=specs,
        out_specs=tuple(VMEM for _ in out_shape) if many else VMEM,
        scratch_shapes=list(scratch),
        compiler_params=pltpu.CompilerParams(vmem_limit_bytes=limit << 20),
        cost_estimate=pl.CostEstimate(flops=0, bytes_accessed=nbytes, transcendentals=0),
    )(*args)


def exchanged(x, axis):
    rows = lax.axis_size(axis)
    sent = x.reshape(rows, x.shape[0] // rows, x.shape[1])
    return lax.all_to_all(sent, axis, 0, 0, tiled=True).reshape(x.shape)


def local(queries, key_cache, value_cache, page_list, shard_counts, out_weight):
    batch, groups, tokens, dim = key_cache.shape
    pages = tokens // PAGE
    shards = lax.axis_size("seq")
    devices = lax.axis_size("head") * shards
    pairs = batch * groups
    heads = groups * (HQ // KVH)
    width = queries.shape[1]
    f32, bf16 = jnp.float32, jnp.bfloat16
    S = jax.ShapeDtypeStruct

    sent = call(
        functools.partial(spread_kernel, shards),
        S((shards, LANES), f32),
        (queries,),
        [VMEM],
        1 << 16,
    )
    live, ends, keys, values = call(
        prepare_kernel,
        (
            S((pairs, LANES), f32),
            S((pairs, pages, 2 * dim), bf16),
            S((pairs, CAP * PAGE, dim), bf16),
            S((pairs, CAP * PAGE, dim), bf16),
        ),
        (shard_counts, page_list, key_cache, value_cache),
        [HBM, HBM, HBM, HBM],
        1 << 23,
        [
            pltpu.VMEM(shard_counts.shape, jnp.int32),
            pltpu.SMEM(page_list.shape, jnp.int32),
            pltpu.VMEM((pairs, tokens, dim), bf16),
            pltpu.VMEM((pairs, tokens, dim), bf16),
            pltpu.SemaphoreType.DMA((2,)),
            pltpu.SemaphoreType.DMA((pairs,)),
            pltpu.SemaphoreType.DMA((pairs,)),
        ],
        53,
    )
    gathered = exchanged(sent, "seq")
    parts, bound = call(
        scores_kernel,
        (S((2 * shards, LANES), f32), S((batch, heads, pages), f32)),
        (live, gathered, ends, keys, values),
        [VMEM, VMEM, VMEM, VMEM, VMEM],
        1 << 20,
    )
    arrived = exchanged(parts, "seq")
    terms = call(project_kernel, S((devices, LANES), f32), (arrived, out_weight), [VMEM, VMEM], 1 << 20)
    landed = exchanged(terms, ("head", "seq"))
    return call(
        finish_kernel,
        (S((batch, width), bf16), S((batch, width), bf16), S((batch, heads, pages), f32)),
        (landed, arrived, bound),
        [VMEM, VMEM, VMEM],
        1 << 18,
    )


def solution(mesh):
    return jax.shard_map(
        local,
        mesh=mesh,
        in_specs=(
            P(None, ("head", "seq")),
            P(None, "head", "seq", None),
            P(None, "head", "seq", None),
            P(None, "head", None),
            P(None, "head", None),
            P(("head", "seq"), None),
        ),
        out_specs=(P(None, ("head", "seq")), P(None, ("head", "seq")), P(None, "head", "seq")),
        check_vma=False,
    )
```

```python
import functools
import math

import jax
import jax.numpy as jnp
from jax import lax
from jax.experimental import pallas as pl
from jax.experimental.pallas import tpu as pltpu
from jax.sharding import PartitionSpec as P

HQ = 64
KVH = 8
HD = 128
PAGE = 16
CAP = 8
SELECT = 256
LANES = 128
NEGATIVE = -1e30
SCALE = 1.0 / math.sqrt(HD)

VMEM = pl.BlockSpec(memory_space=pltpu.VMEM)
HBM = pl.BlockSpec(memory_space=pltpu.HBM)


def block_lanes(shape, width):
    return lax.broadcasted_iota(jnp.int32, shape, 1) // width


def spread_kernel(copies, query_ref, out_ref):
    rows = query_ref[...].astype(jnp.float32)
    line = jnp.concatenate([rows[b : b + 1, :] for b in range(rows.shape[0])], axis=1)
    out_ref[...] = jnp.broadcast_to(line, (copies, LANES))


def prepare_kernel(
    lists_hbm, key_hbm, value_hbm,
    live_ref, ends_ref, keys_out, values_out,
    lists_ref, pages_ref, offset_ref, spot_ref, wide_ref, key_ref, value_ref, list_sems, key_sems, value_sems,
):
    batch, groups, tokens, dim = key_hbm.shape
    pages = tokens // PAGE
    shard = lax.axis_index("seq")
    pairs = [(b, g) for b in range(batch) for g in range(groups)]
    lists = [
        pltpu.make_async_copy(lists_hbm, lists_ref, list_sems.at[0]),
        pltpu.make_async_copy(lists_hbm, pages_ref, list_sems.at[1]),
    ]
    key_copies = [
        pltpu.make_async_copy(key_hbm.at[b, g], key_ref.at[n], key_sems.at[n])
        for n, (b, g) in enumerate(pairs)
    ]
    value_copies = [
        pltpu.make_async_copy(value_hbm.at[b, g], value_ref.at[n], value_sems.at[n])
        for n, (b, g) in enumerate(pairs)
    ]
    for copy in lists + key_copies + value_copies:
        copy.start()
    lists[0].wait()
    for n, (b, g) in enumerate(pairs):
        line = lists_ref[b, g : g + 1, :]
        index = lax.broadcasted_iota(jnp.int32, line.shape, 1) - SELECT
        earlier = jnp.where((index >= 0) & (index < shard), line, 0)
        count = jnp.sum(jnp.where(index == shard, line, 0), axis=1, keepdims=True)
        lanes = lax.broadcasted_iota(jnp.int32, (1, LANES), 1)
        live_ref[n : n + 1, :] = jnp.where(lanes // PAGE < count, 1.0, 0.0)
        offset = jnp.sum(earlier, axis=1, keepdims=True)
        offset_ref[n : n + 1, :] = jnp.broadcast_to(offset, (1, LANES))
    offsets = pltpu.make_async_copy(offset_ref, spot_ref, list_sems.at[2])
    offsets.start()
    for n in range(len(pairs)):
        key_copies[n].wait()
        wide_ref[...] = key_ref[n].astype(jnp.float32)
        largest = wide_ref[pl.ds(0, pages, stride=PAGE), :]
        smallest = largest
        for row in range(1, PAGE):
            other = wide_ref[pl.ds(row, pages, stride=PAGE), :]
            largest = jnp.maximum(largest, other)
            smallest = jnp.minimum(smallest, other)
        ends_ref[n, :, :dim] = largest.astype(jnp.bfloat16)
        ends_ref[n, :, dim:] = smallest.astype(jnp.bfloat16)
    lists[1].wait()
    offsets.wait()
    for n, (b, g) in enumerate(pairs):
        value_copies[n].wait()
        for slot in range(CAP):
            at = jnp.minimum(spot_ref[n, 0] + slot, SELECT - 1)
            page = jnp.clip(pages_ref[b, g, at] - shard * pages, 0, pages - 1)
            start = pl.multiple_of(page * PAGE, PAGE)
            rows = slice(slot * PAGE, (slot + 1) * PAGE)
            keys_out[n, rows, :] = key_ref[n, pl.ds(start, PAGE), :]
            values_out[n, rows, :] = value_ref[n, pl.ds(start, PAGE), :]


def scores_kernel(live_ref, query_ref, ends_ref, keys_ref, values_ref, part_ref, bound_ref):
    batch, heads, _ = bound_ref.shape
    groups = live_ref.shape[0] // batch
    group = heads // groups
    width = LANES // 4
    quarters = [query_ref[pl.ds(q, heads, stride=4), :] for q in range(4)]
    lane_block = block_lanes((heads, LANES), width)

    def rows_of(b):
        found = jnp.zeros((heads, LANES), jnp.float32)
        for q in range(4):
            shift = (q - b) * width % LANES
            moved = pltpu.roll(quarters[q], shift, 1) if shift else quarters[q]
            found = jnp.where(lane_block == q, moved, found)
        return found

    lanes = lax.broadcasted_iota(jnp.int32, (group, LANES), 1)
    subs = lax.broadcasted_iota(jnp.int32, (group, LANES), 0)
    page_row = jnp.zeros((group, LANES), jnp.float32)
    head_rows = [jnp.zeros((group, LANES), jnp.float32) for _ in range(groups)]
    mixed = []
    contract = (((1,), (1,)), ((), ()))
    for b in range(batch):
        rows = rows_of(b)
        parts = []
        for g in range(groups):
            n = b * groups + g
            query = rows[g * group : (g + 1) * group]
            signed = jnp.concatenate([jnp.maximum(query, 0.0), jnp.minimum(query, 0.0)], axis=1)
            bound = SCALE * lax.dot_general(
                signed.astype(jnp.bfloat16), ends_ref[n], contract, preferred_element_type=jnp.float32
            )
            bound_ref[b, g * group : (g + 1) * group, :] = bound
            peak = jnp.max(bound, axis=1, keepdims=True)
            mass = jnp.sum(jnp.exp(bound - peak), axis=1, keepdims=True)
            page_row = jnp.where(lanes == subs * (batch * groups) + n, peak + jnp.log(mass), page_row)
            scores = SCALE * lax.dot_general(
                query.astype(jnp.bfloat16), keys_ref[n], contract, preferred_element_type=jnp.float32
            )
            live = live_ref[n : n + 1, :] > 0.0
            scores = jnp.where(live, scores, NEGATIVE)
            top = jnp.max(scores, axis=1, keepdims=True)
            weights = jnp.where(live, jnp.exp(scores - top), 0.0)
            total = jnp.maximum(jnp.sum(weights, axis=1, keepdims=True), 1e-30)
            unnormed = jnp.dot(
                weights.astype(jnp.bfloat16), values_ref[n], preferred_element_type=jnp.float32
            )
            parts.append(unnormed / total)
            head_rows[g] = jnp.where(
                lanes == LANES // 2 + b, top + jnp.log(total), head_rows[g]
            )
        mixed.append(jnp.concatenate(parts, axis=0))
    page_line = jnp.sum(page_row, axis=0, keepdims=True)
    seconds = jnp.concatenate(head_rows, axis=0) + page_line
    for q in range(4):
        line = jnp.zeros((heads, LANES), jnp.float32)
        for b in range(batch):
            shift = (b - q) * width % LANES
            moved = pltpu.roll(mixed[b], shift, 1) if shift else mixed[b]
            line = jnp.where(lane_block == b, moved, line)
        part_ref[pl.ds(2 * q, heads, stride=8), :] = line
        part_ref[pl.ds(2 * q + 1, heads, stride=8), :] = seconds


def merged_line(part_ref):
    shards = part_ref.shape[0] // 2
    values = part_ref[pl.ds(0, shards, stride=2), :]
    logs = part_ref[pl.ds(1, shards, stride=2), :]
    shares = jnp.exp(logs - jnp.max(logs, axis=0, keepdims=True))
    block = block_lanes((shards, LANES), LANES // 4)
    spread = jnp.zeros((shards, LANES), jnp.float32)
    for b in range(4):
        at = LANES // 2 + b
        spread = jnp.where(block == b, shares[:, at : at + 1], spread)
    line = jnp.sum(spread * values, axis=0, keepdims=True) / jnp.sum(spread, axis=0, keepdims=True)
    return line.astype(jnp.bfloat16)


def project_kernel(part_ref, weight_ref, out_ref):
    width = LANES // 4
    columns = weight_ref.shape[1]
    chunk = 4 * LANES
    line = merged_line(part_ref).astype(jnp.float32)
    rows = [line[:, b * width : (b + 1) * width] for b in range(4)]
    small = lax.broadcasted_iota(jnp.int32, (8, width), 0)
    sides = []
    for d in range(4):
        side = jnp.zeros((8, width), jnp.float32)
        for b in range(4):
            side = jnp.where((small + d) % 4 == b, rows[b], side)
        sides.append(side)
    left = jnp.concatenate(sides, axis=0).astype(jnp.bfloat16)
    subs = lax.broadcasted_iota(jnp.int32, (8, LANES), 0)
    block = block_lanes((8, LANES), width)
    for start in range(0, columns, chunk):
        terms = jnp.dot(left, weight_ref[:, start : start + chunk], preferred_element_type=jnp.float32)
        for pair in range(0, chunk, 2 * LANES):
            found = jnp.zeros((8, LANES), jnp.float32)
            for d in range(4):
                turn = terms[8 * d : 8 * (d + 1), pair : pair + 2 * LANES]
                turn = jnp.where(subs < 4, turn[:, :LANES], turn[:, LANES:])
                turn = pltpu.roll(turn, d * width, 1) if d else turn
                found = jnp.where(block == (subs + d) % 4, turn, found)
            at = (start + pair) // width
            out_ref[at : at + 8, :] = found


def finish_kernel(terms_ref, part_ref, bound_ref, output_ref, attention_ref, mass_ref):
    batch, heads, pages = bound_ref.shape
    shards = part_ref.shape[0] // 2
    group = HQ // KVH
    groups = heads // group
    width = LANES // 4
    sums = jnp.sum(terms_ref[...], axis=0, keepdims=True)
    attention = merged_line(part_ref)
    for b in range(batch):
        columns = slice(b * width, (b + 1) * width)
        output_ref[b : b + 1, :] = sums[:, columns].astype(jnp.bfloat16)
        attention_ref[b : b + 1, :] = attention[:, columns]
    logs = part_ref[pl.ds(1, shards, stride=2), :]
    peak = jnp.max(logs, axis=0, keepdims=True)
    line = peak + jnp.log(jnp.sum(jnp.exp(logs - peak), axis=0, keepdims=True))
    lanes = lax.broadcasted_iota(jnp.int32, (group, LANES), 1)
    subs = lax.broadcasted_iota(jnp.int32, (group, LANES), 0)
    for b in range(batch):
        for g in range(groups):
            n = b * groups + g
            column = jnp.sum(
                jnp.where(lanes == subs * (batch * groups) + n, line, 0.0), axis=1, keepdims=True
            )
            rows = slice(g * group, (g + 1) * group)
            mass_ref[b, rows, :] = jnp.exp(bound_ref[b, rows, :] - column)


def call(kernel, out_shape, args, specs, nbytes, scratch=(), limit=32):
    many = isinstance(out_shape, tuple)
    return pl.pallas_call(
        kernel,
        out_shape=out_shape,
        in_specs=specs,
        out_specs=tuple(VMEM for _ in out_shape) if many else VMEM,
        scratch_shapes=list(scratch),
        compiler_params=pltpu.CompilerParams(vmem_limit_bytes=limit << 20),
        cost_estimate=pl.CostEstimate(flops=0, bytes_accessed=nbytes, transcendentals=0),
    )(*args)


def exchanged(x, axis):
    rows = lax.axis_size(axis)
    sent = x.reshape(rows, x.shape[0] // rows, x.shape[1])
    return lax.all_to_all(sent, axis, 0, 0, tiled=True).reshape(x.shape)


def local(queries, key_cache, value_cache, page_list, shard_counts, out_weight):
    batch, groups, tokens, dim = key_cache.shape
    pages = tokens // PAGE
    shards = lax.axis_size("seq")
    devices = lax.axis_size("head") * shards
    pairs = batch * groups
    heads = groups * (HQ // KVH)
    width = queries.shape[1]
    f32, bf16 = jnp.float32, jnp.bfloat16
    S = jax.ShapeDtypeStruct

    sent = call(
        functools.partial(spread_kernel, shards),
        S((shards, LANES), f32),
        (queries,),
        [VMEM],
        1 << 16,
    )
    sent, page_list, shard_counts = lax.optimization_barrier((sent, page_list, shard_counts))
    lists = jnp.concatenate([page_list, shard_counts], axis=2)
    live, ends, keys, values = call(
        prepare_kernel,
        (
            S((pairs, LANES), f32),
            S((pairs, pages, 2 * dim), bf16),
            S((pairs, CAP * PAGE, dim), bf16),
            S((pairs, CAP * PAGE, dim), bf16),
        ),
        (lists, key_cache, value_cache),
        [HBM, HBM, HBM],
        1 << 23,
        [
            pltpu.VMEM(lists.shape, jnp.int32),
            pltpu.SMEM(lists.shape, jnp.int32),
            pltpu.VMEM((pairs, LANES), jnp.int32),
            pltpu.SMEM((pairs, LANES), jnp.int32),
            pltpu.VMEM((tokens, dim), f32),
            pltpu.VMEM((pairs, tokens, dim), bf16),
            pltpu.VMEM((pairs, tokens, dim), bf16),
            pltpu.SemaphoreType.DMA((3,)),
            pltpu.SemaphoreType.DMA((pairs,)),
            pltpu.SemaphoreType.DMA((pairs,)),
        ],
        53,
    )
    gathered = exchanged(sent, "seq")
    parts, bound = call(
        scores_kernel,
        (S((2 * shards, LANES), f32), S((batch, heads, pages), f32)),
        (live, gathered, ends, keys, values),
        [VMEM, VMEM, VMEM, VMEM, VMEM],
        1 << 20,
    )
    arrived = exchanged(parts, "seq")
    terms = call(project_kernel, S((devices, LANES), f32), (arrived, out_weight), [VMEM, VMEM], 1 << 20)
    landed = exchanged(terms, ("head", "seq"))
    return call(
        finish_kernel,
        (S((batch, width), bf16), S((batch, width), bf16), S((batch, heads, pages), f32)),
        (landed, arrived, bound),
        [VMEM, VMEM, VMEM],
        1 << 18,
    )


def solution(mesh):
    return jax.shard_map(
        local,
        mesh=mesh,
        in_specs=(
            P(None, ("head", "seq")),
            P(None, "head", "seq", None),
            P(None, "head", "seq", None),
            P(None, "head", None),
            P(None, "head", None),
            P(("head", "seq"), None),
        ),
        out_specs=(P(None, ("head", "seq")), P(None, ("head", "seq")), P(None, "head", "seq")),
        check_vma=False,
    )
```

```python
import functools
import math

import jax
import jax.numpy as jnp
from jax import lax
from jax.experimental import pallas as pl
from jax.experimental.pallas import tpu as pltpu
from jax.sharding import PartitionSpec as P

HQ = 64
KVH = 8
HD = 128
PAGE = 16
CAP = 8
SELECT = 256
LANES = 128
NEGATIVE = -1e30
SCALE = 1.0 / math.sqrt(HD)

VMEM = pl.BlockSpec(memory_space=pltpu.VMEM)
HBM = pl.BlockSpec(memory_space=pltpu.HBM)


def block_lanes(shape, width):
    return lax.broadcasted_iota(jnp.int32, shape, 1) // width


def spread_kernel(copies, query_ref, out_ref):
    rows = query_ref[...].astype(jnp.float32)
    line = jnp.concatenate([rows[b : b + 1, :] for b in range(rows.shape[0])], axis=1)
    out_ref[...] = jnp.broadcast_to(line, (copies, LANES))


def prepare_kernel(
    lists_ref, key_hbm,
    live_ref, start_ref, ends_ref, keys_out,
    spot_ref, wide_ref, key_ref, spot_sem, key_sems,
):
    batch, groups, tokens, dim = key_hbm.shape
    pages = tokens // PAGE
    shard = lax.axis_index("seq")
    pairs = [(b, g) for b in range(batch) for g in range(groups)]
    key_copies = [
        pltpu.make_async_copy(key_hbm.at[b, g], key_ref.at[n], key_sems.at[n])
        for n, (b, g) in enumerate(pairs)
    ]
    for copy in key_copies:
        copy.start()
    lists = jnp.concatenate([lists_ref[b] for b in range(batch)], axis=0)
    listed, counts = lists[:, :SELECT], lists[:, SELECT:]
    index = lax.broadcasted_iota(jnp.int32, counts.shape, 1)
    offset = jnp.sum(jnp.where(index < shard, counts, 0), axis=1, keepdims=True)
    count = jnp.sum(jnp.where(index == shard, counts, 0), axis=1, keepdims=True)
    lanes = lax.broadcasted_iota(jnp.int32, (len(pairs), LANES), 1)
    live_ref[...] = jnp.where(lanes // PAGE < count, 1.0, 0.0)
    place = lax.broadcasted_iota(jnp.int32, listed.shape, 1)
    page = jnp.zeros((len(pairs), LANES), jnp.int32)
    for slot in range(CAP):
        found = jnp.sum(jnp.where(place == offset + slot, listed, 0), axis=1, keepdims=True)
        page = jnp.where(lanes == slot, found, page)
    start_ref[...] = jnp.clip(page - shard * pages, 0, pages - 1) * PAGE
    spots = pltpu.make_async_copy(start_ref, spot_ref, spot_sem)
    spots.start()
    for n in range(len(pairs)):
        key_copies[n].wait()
        wide_ref[...] = key_ref[n].astype(jnp.float32)
        largest = wide_ref[pl.ds(0, pages, stride=PAGE), :]
        smallest = largest
        for row in range(1, PAGE):
            other = wide_ref[pl.ds(row, pages, stride=PAGE), :]
            largest = jnp.maximum(largest, other)
            smallest = jnp.minimum(smallest, other)
        ends_ref[n, :, :dim] = largest.astype(jnp.bfloat16)
        ends_ref[n, :, dim:] = smallest.astype(jnp.bfloat16)
    spots.wait()
    starts = [
        [pl.multiple_of(spot_ref[n, slot], PAGE) for slot in range(CAP)] for n in range(len(pairs))
    ]
    for n in range(len(pairs)):
        for slot in range(CAP):
            rows = slice(slot * PAGE, (slot + 1) * PAGE)
            keys_out[n, rows, :] = key_ref[n, pl.ds(starts[n][slot], PAGE), :]


def scores_kernel(
    live_ref, start_ref, query_ref, ends_ref, keys_ref, value_ref,
    part_ref, bound_ref,
    spot_ref, spot_sem,
):
    spots = pltpu.make_async_copy(start_ref, spot_ref, spot_sem)
    spots.start()
    batch, heads, _ = bound_ref.shape
    groups = live_ref.shape[0] // batch
    group = heads // groups
    width = LANES // 4
    quarters = [query_ref[pl.ds(q, heads, stride=4), :] for q in range(4)]
    lane_block = block_lanes((heads, LANES), width)

    def rows_of(b):
        found = jnp.zeros((heads, LANES), jnp.float32)
        for q in range(4):
            shift = (q - b) * width % LANES
            moved = pltpu.roll(quarters[q], shift, 1) if shift else quarters[q]
            found = jnp.where(lane_block == q, moved, found)
        return found

    lanes = lax.broadcasted_iota(jnp.int32, (group, LANES), 1)
    subs = lax.broadcasted_iota(jnp.int32, (group, LANES), 0)
    page_row = jnp.zeros((group, LANES), jnp.float32)
    head_rows = [jnp.zeros((group, LANES), jnp.float32) for _ in range(groups)]
    shares = []
    contract = (((1,), (1,)), ((), ()))
    for b in range(batch):
        rows = rows_of(b)
        for g in range(groups):
            n = b * groups + g
            query = rows[g * group : (g + 1) * group]
            signed = jnp.concatenate([jnp.maximum(query, 0.0), jnp.minimum(query, 0.0)], axis=1)
            bound = SCALE * lax.dot_general(
                signed.astype(jnp.bfloat16), ends_ref[n], contract, preferred_element_type=jnp.float32
            )
            bound_ref[b, g * group : (g + 1) * group, :] = bound
            peak = jnp.max(bound, axis=1, keepdims=True)
            mass = jnp.sum(jnp.exp(bound - peak), axis=1, keepdims=True)
            page_row = jnp.where(lanes == subs * (batch * groups) + n, peak + jnp.log(mass), page_row)
            scores = SCALE * lax.dot_general(
                query.astype(jnp.bfloat16), keys_ref[n], contract, preferred_element_type=jnp.float32
            )
            live = live_ref[n : n + 1, :] > 0.0
            scores = jnp.where(live, scores, NEGATIVE)
            top = jnp.max(scores, axis=1, keepdims=True)
            weights = jnp.where(live, jnp.exp(scores - top), 0.0)
            total = jnp.maximum(jnp.sum(weights, axis=1, keepdims=True), 1e-30)
            shares.append((weights.astype(jnp.bfloat16), total))
            head_rows[g] = jnp.where(
                lanes == LANES // 2 + b, top + jnp.log(total), head_rows[g]
            )
    spots.wait()
    mixed = []
    for b in range(batch):
        parts = []
        for g in range(groups):
            n = b * groups + g
            weights, total = shares[n]
            values = jnp.concatenate(
                [
                    value_ref[b, g, pl.ds(pl.multiple_of(spot_ref[n, slot], PAGE), PAGE), :]
                    for slot in range(CAP)
                ],
                axis=0,
            )
            parts.append(jnp.dot(weights, values, preferred_element_type=jnp.float32) / total)
        mixed.append(jnp.concatenate(parts, axis=0))
    page_line = jnp.sum(page_row, axis=0, keepdims=True)
    seconds = jnp.concatenate(head_rows, axis=0) + page_line
    for q in range(4):
        line = jnp.zeros((heads, LANES), jnp.float32)
        for b in range(batch):
            shift = (b - q) * width % LANES
            moved = pltpu.roll(mixed[b], shift, 1) if shift else mixed[b]
            line = jnp.where(lane_block == b, moved, line)
        part_ref[pl.ds(2 * q, heads, stride=8), :] = line
        part_ref[pl.ds(2 * q + 1, heads, stride=8), :] = seconds


def merged_line(part_ref):
    shards = part_ref.shape[0] // 2
    values = part_ref[pl.ds(0, shards, stride=2), :]
    logs = part_ref[pl.ds(1, shards, stride=2), :]
    shares = jnp.exp(logs - jnp.max(logs, axis=0, keepdims=True))
    block = block_lanes((shards, LANES), LANES // 4)
    spread = jnp.zeros((shards, LANES), jnp.float32)
    for b in range(4):
        at = LANES // 2 + b
        spread = jnp.where(block == b, shares[:, at : at + 1], spread)
    line = jnp.sum(spread * values, axis=0, keepdims=True) / jnp.sum(spread, axis=0, keepdims=True)
    return line.astype(jnp.bfloat16)


def project_kernel(part_ref, weight_ref, out_ref):
    width = LANES // 4
    columns = weight_ref.shape[1]
    chunk = 4 * LANES
    line = merged_line(part_ref).astype(jnp.float32)
    rows = [line[:, b * width : (b + 1) * width] for b in range(4)]
    small = lax.broadcasted_iota(jnp.int32, (8, width), 0)
    sides = []
    for d in range(4):
        side = jnp.zeros((8, width), jnp.float32)
        for b in range(4):
            side = jnp.where((small + d) % 4 == b, rows[b], side)
        sides.append(side)
    left = jnp.concatenate(sides, axis=0).astype(jnp.bfloat16)
    subs = lax.broadcasted_iota(jnp.int32, (8, LANES), 0)
    block = block_lanes((8, LANES), width)
    for start in range(0, columns, chunk):
        terms = jnp.dot(left, weight_ref[:, start : start + chunk], preferred_element_type=jnp.float32)
        for pair in range(0, chunk, 2 * LANES):
            found = jnp.zeros((8, LANES), jnp.float32)
            for d in range(4):
                turn = terms[8 * d : 8 * (d + 1), pair : pair + 2 * LANES]
                turn = jnp.where(subs < 4, turn[:, :LANES], turn[:, LANES:])
                turn = pltpu.roll(turn, d * width, 1) if d else turn
                found = jnp.where(block == (subs + d) % 4, turn, found)
            at = (start + pair) // width
            out_ref[at : at + 8, :] = found


def finish_kernel(terms_ref, part_ref, bound_ref, output_ref, attention_ref, mass_ref):
    batch, heads, pages = bound_ref.shape
    shards = part_ref.shape[0] // 2
    group = HQ // KVH
    groups = heads // group
    width = LANES // 4
    sums = jnp.sum(terms_ref[...], axis=0, keepdims=True)
    attention = merged_line(part_ref)
    for b in range(batch):
        columns = slice(b * width, (b + 1) * width)
        output_ref[b : b + 1, :] = sums[:, columns].astype(jnp.bfloat16)
        attention_ref[b : b + 1, :] = attention[:, columns]
    logs = part_ref[pl.ds(1, shards, stride=2), :]
    peak = jnp.max(logs, axis=0, keepdims=True)
    line = peak + jnp.log(jnp.sum(jnp.exp(logs - peak), axis=0, keepdims=True))
    lanes = lax.broadcasted_iota(jnp.int32, (group, LANES), 1)
    subs = lax.broadcasted_iota(jnp.int32, (group, LANES), 0)
    for b in range(batch):
        for g in range(groups):
            n = b * groups + g
            column = jnp.sum(
                jnp.where(lanes == subs * (batch * groups) + n, line, 0.0), axis=1, keepdims=True
            )
            rows = slice(g * group, (g + 1) * group)
            mass_ref[b, rows, :] = jnp.exp(bound_ref[b, rows, :] - column)


def call(kernel, out_shape, args, specs, nbytes, scratch=(), limit=32):
    many = isinstance(out_shape, tuple)
    return pl.pallas_call(
        kernel,
        out_shape=out_shape,
        in_specs=specs,
        out_specs=tuple(VMEM for _ in out_shape) if many else VMEM,
        scratch_shapes=list(scratch),
        compiler_params=pltpu.CompilerParams(vmem_limit_bytes=limit << 20),
        cost_estimate=pl.CostEstimate(flops=0, bytes_accessed=nbytes, transcendentals=0),
    )(*args)


def exchanged(x, axis):
    rows = lax.axis_size(axis)
    sent = x.reshape(rows, x.shape[0] // rows, x.shape[1])
    return lax.all_to_all(sent, axis, 0, 0, tiled=True).reshape(x.shape)


def local(queries, key_cache, value_cache, page_list, shard_counts, out_weight):
    batch, groups, tokens, dim = key_cache.shape
    pages = tokens // PAGE
    shards = lax.axis_size("seq")
    devices = lax.axis_size("head") * shards
    pairs = batch * groups
    heads = groups * (HQ // KVH)
    width = queries.shape[1]
    f32, bf16 = jnp.float32, jnp.bfloat16
    S = jax.ShapeDtypeStruct

    sent = call(
        functools.partial(spread_kernel, shards),
        S((shards, LANES), f32),
        (queries,),
        [VMEM],
        1 << 16,
    )
    sent, page_list, shard_counts = lax.optimization_barrier((sent, page_list, shard_counts))
    lists = jnp.concatenate([page_list, shard_counts], axis=2)
    live, starts, ends, keys = call(
        prepare_kernel,
        (
            S((pairs, LANES), f32),
            S((pairs, LANES), jnp.int32),
            S((pairs, pages, 2 * dim), bf16),
            S((pairs, CAP * PAGE, dim), bf16),
        ),
        (lists, key_cache),
        [VMEM, HBM],
        1 << 22,
        [
            pltpu.SMEM((pairs, LANES), jnp.int32),
            pltpu.VMEM((tokens, dim), f32),
            pltpu.VMEM((pairs, tokens, dim), bf16),
            pltpu.SemaphoreType.DMA,
            pltpu.SemaphoreType.DMA((pairs,)),
        ],
        52,
    )
    gathered = exchanged(sent, "seq")
    parts, bound = call(
        scores_kernel,
        (S((2 * shards, LANES), f32), S((batch, heads, pages), f32)),
        (live, starts, gathered, ends, keys, value_cache),
        [VMEM, VMEM, VMEM, VMEM, VMEM, VMEM],
        1 << 20,
        [pltpu.SMEM((pairs, LANES), jnp.int32), pltpu.SemaphoreType.DMA],
    )
    arrived = exchanged(parts, "seq")
    terms = call(project_kernel, S((devices, LANES), f32), (arrived, out_weight), [VMEM, VMEM], 1 << 20)
    landed = exchanged(terms, ("head", "seq"))
    return call(
        finish_kernel,
        (S((batch, width), bf16), S((batch, width), bf16), S((batch, heads, pages), f32)),
        (landed, arrived, bound),
        [VMEM, VMEM, VMEM],
        1 << 18,
    )


def solution(mesh):
    return jax.shard_map(
        local,
        mesh=mesh,
        in_specs=(
            P(None, ("head", "seq")),
            P(None, "head", "seq", None),
            P(None, "head", "seq", None),
            P(None, "head", None),
            P(None, "head", None),
            P(("head", "seq"), None),
        ),
        out_specs=(P(None, ("head", "seq")), P(None, ("head", "seq")), P(None, "head", "seq")),
        check_vma=False,
    )
```

```python
import functools
import math

import jax
import jax.numpy as jnp
from jax import lax
from jax.experimental import pallas as pl
from jax.experimental.pallas import tpu as pltpu
from jax.sharding import PartitionSpec as P

HQ = 64
KVH = 8
HD = 128
PAGE = 16
CAP = 8
SELECT = 256
LANES = 128
NEGATIVE = -1e30
SCALE = 1.0 / math.sqrt(HD)

VMEM = pl.BlockSpec(memory_space=pltpu.VMEM)
HBM = pl.BlockSpec(memory_space=pltpu.HBM)


def block_lanes(shape, width):
    return lax.broadcasted_iota(jnp.int32, shape, 1) // width


def spread_kernel(copies, query_ref, out_ref):
    rows = query_ref[...].astype(jnp.float32)
    line = jnp.concatenate([rows[b : b + 1, :] for b in range(rows.shape[0])], axis=1)
    out_ref[...] = jnp.broadcast_to(line, (copies, LANES))


def folded_rows(pieces, combine):
    rows = lax.broadcasted_iota(jnp.int32, pieces[0].shape, 0)

    def step(first, second, keep, shift):
        kept = jnp.where(keep, first, second)
        other = jnp.where(keep, second, first)
        return combine(kept, pltpu.roll(other, shift, 0))

    def four(a, b, c, d, turn):
        at = (rows + turn) % 8
        left = step(a, b, at < 4, 4)
        right = step(c, d, (at < 2) | (at >= 6), 4)
        return step(left, right, at % 4 >= 2, 2)

    odd = four(pieces[3], pieces[7], pieces[1], pieces[5], 0)
    even = four(pieces[2], pieces[6], pieces[0], pieces[4], 1)
    return step(odd, even, rows % 2 == 1, 1)


def prepare_kernel(
    lists_ref, key_hbm,
    live_ref, start_ref, ends_ref, keys_out,
    spot_ref, key_ref, spot_sem, key_sems,
):
    batch, groups, tokens, dim = key_hbm.shape
    pages = tokens // PAGE
    shard = lax.axis_index("seq")
    pairs = [(b, g) for b in range(batch) for g in range(groups)]
    key_copies = [
        pltpu.make_async_copy(key_hbm.at[b, g], key_ref.at[n], key_sems.at[n])
        for n, (b, g) in enumerate(pairs)
    ]
    for copy in key_copies:
        copy.start()
    lists = jnp.concatenate([lists_ref[b] for b in range(batch)], axis=0).astype(jnp.float32)
    listed, counts = lists[:, :SELECT], lists[:, SELECT:]
    index = lax.broadcasted_iota(jnp.int32, counts.shape, 1)
    offset = jnp.sum(jnp.where(index < shard, counts, 0.0), axis=1, keepdims=True).astype(jnp.int32)
    count = jnp.sum(jnp.where(index == shard, counts, 0.0), axis=1, keepdims=True).astype(jnp.int32)
    lanes = lax.broadcasted_iota(jnp.int32, (len(pairs), LANES), 1)
    live_ref[...] = jnp.where(lanes // PAGE < count, 1.0, 0.0)
    place = lax.broadcasted_iota(jnp.int32, listed.shape, 1)
    page = jnp.zeros((len(pairs), LANES), jnp.float32)
    for slot in range(CAP):
        found = jnp.sum(jnp.where(place == offset + slot, listed, 0.0), axis=1, keepdims=True)
        page = jnp.where(lanes == slot, found, page)
    start_ref[...] = jnp.clip(page.astype(jnp.int32) - shard * pages, 0, pages - 1) * PAGE
    spots = pltpu.make_async_copy(start_ref, spot_ref, spot_sem)
    spots.start()
    for n in range(len(pairs)):
        key_copies[n].wait()
        for first in range(0, pages, 16):
            largest, smallest = [], []
            for half in (first, first + 8):
                wide = key_ref[n, half * PAGE : (half + 8) * PAGE, :].astype(jnp.float32)
                parts = [wide[8 * k : 8 * (k + 1)] for k in range(PAGE)]
                above = [jnp.maximum(parts[2 * k], parts[2 * k + 1]) for k in range(8)]
                below = [jnp.minimum(parts[2 * k], parts[2 * k + 1]) for k in range(8)]
                largest.append(folded_rows(above, jnp.maximum))
                smallest.append(folded_rows(below, jnp.minimum))
            at = slice(first, first + 16)
            ends_ref[n, at, :dim] = jnp.concatenate(largest, axis=0).astype(jnp.bfloat16)
            ends_ref[n, at, dim:] = jnp.concatenate(smallest, axis=0).astype(jnp.bfloat16)
    spots.wait()
    starts = [
        [pl.multiple_of(spot_ref[n, slot], PAGE) for slot in range(CAP)] for n in range(len(pairs))
    ]
    for n in range(len(pairs)):
        for slot in range(CAP):
            rows = slice(slot * PAGE, (slot + 1) * PAGE)
            keys_out[n, rows, :] = key_ref[n, pl.ds(starts[n][slot], PAGE), :]


def scores_kernel(
    live_ref, start_ref, query_ref, ends_ref, keys_ref, value_ref,
    part_ref, bound_ref,
    spot_ref, spot_sem,
):
    spots = pltpu.make_async_copy(start_ref, spot_ref, spot_sem)
    spots.start()
    batch, heads, _ = bound_ref.shape
    groups = live_ref.shape[0] // batch
    group = heads // groups
    width = LANES // 4
    quarters = [query_ref[pl.ds(q, heads, stride=4), :] for q in range(4)]
    lane_block = block_lanes((heads, LANES), width)

    def rows_of(b):
        found = jnp.zeros((heads, LANES), jnp.float32)
        for q in range(4):
            shift = (q - b) * width % LANES
            moved = pltpu.roll(quarters[q], shift, 1) if shift else quarters[q]
            found = jnp.where(lane_block == q, moved, found)
        return found

    lanes = lax.broadcasted_iota(jnp.int32, (group, LANES), 1)
    subs = lax.broadcasted_iota(jnp.int32, (group, LANES), 0)
    page_row = jnp.zeros((group, LANES), jnp.float32)
    head_rows = [jnp.zeros((group, LANES), jnp.float32) for _ in range(groups)]
    shares = []
    contract = (((1,), (1,)), ((), ()))
    for b in range(batch):
        rows = rows_of(b)
        for g in range(groups):
            n = b * groups + g
            query = rows[g * group : (g + 1) * group]
            signed = jnp.concatenate([jnp.maximum(query, 0.0), jnp.minimum(query, 0.0)], axis=1)
            bound = SCALE * lax.dot_general(
                signed.astype(jnp.bfloat16), ends_ref[n], contract, preferred_element_type=jnp.float32
            )
            bound_ref[b, g * group : (g + 1) * group, :] = bound
            peak = jnp.max(bound, axis=1, keepdims=True)
            mass = jnp.sum(jnp.exp(bound - peak), axis=1, keepdims=True)
            page_row = jnp.where(lanes == subs * (batch * groups) + n, peak + jnp.log(mass), page_row)
            scores = SCALE * lax.dot_general(
                query.astype(jnp.bfloat16), keys_ref[n], contract, preferred_element_type=jnp.float32
            )
            live = live_ref[n : n + 1, :] > 0.0
            scores = jnp.where(live, scores, NEGATIVE)
            top = jnp.max(scores, axis=1, keepdims=True)
            weights = jnp.where(live, jnp.exp(scores - top), 0.0)
            total = jnp.maximum(jnp.sum(weights, axis=1, keepdims=True), 1e-30)
            shares.append((weights.astype(jnp.bfloat16), total))
            head_rows[g] = jnp.where(
                lanes == LANES // 2 + b, top + jnp.log(total), head_rows[g]
            )
    spots.wait()
    mixed = []
    for b in range(batch):
        parts = []
        for g in range(groups):
            n = b * groups + g
            weights, total = shares[n]
            values = jnp.concatenate(
                [
                    value_ref[b, g, pl.ds(pl.multiple_of(spot_ref[n, slot], PAGE), PAGE), :]
                    for slot in range(CAP)
                ],
                axis=0,
            )
            parts.append(jnp.dot(weights, values, preferred_element_type=jnp.float32) / total)
        mixed.append(jnp.concatenate(parts, axis=0))
    page_line = jnp.sum(page_row, axis=0, keepdims=True)
    seconds = jnp.concatenate(head_rows, axis=0) + page_line
    for q in range(4):
        line = jnp.zeros((heads, LANES), jnp.float32)
        for b in range(batch):
            shift = (b - q) * width % LANES
            moved = pltpu.roll(mixed[b], shift, 1) if shift else mixed[b]
            line = jnp.where(lane_block == b, moved, line)
        part_ref[pl.ds(2 * q, heads, stride=8), :] = line
        part_ref[pl.ds(2 * q + 1, heads, stride=8), :] = seconds


def merged_line(part_ref):
    shards = part_ref.shape[0] // 2
    values = part_ref[pl.ds(0, shards, stride=2), :]
    logs = part_ref[pl.ds(1, shards, stride=2), :]
    shares = jnp.exp(logs - jnp.max(logs, axis=0, keepdims=True))
    block = block_lanes((shards, LANES), LANES // 4)
    spread = jnp.zeros((shards, LANES), jnp.float32)
    for b in range(4):
        at = LANES // 2 + b
        spread = jnp.where(block == b, shares[:, at : at + 1], spread)
    line = jnp.sum(spread * values, axis=0, keepdims=True) / jnp.sum(spread, axis=0, keepdims=True)
    return line.astype(jnp.bfloat16)


def project_kernel(part_ref, weight_ref, out_ref):
    width = LANES // 4
    columns = weight_ref.shape[1]
    chunk = 4 * LANES
    line = merged_line(part_ref).astype(jnp.float32)
    rows = [line[:, b * width : (b + 1) * width] for b in range(4)]
    small = lax.broadcasted_iota(jnp.int32, (8, width), 0)
    sides = []
    for d in range(4):
        side = jnp.zeros((8, width), jnp.float32)
        for b in range(4):
            side = jnp.where((small + d) % 4 == b, rows[b], side)
        sides.append(side)
    left = jnp.concatenate(sides, axis=0).astype(jnp.bfloat16)
    subs = lax.broadcasted_iota(jnp.int32, (8, LANES), 0)
    block = block_lanes((8, LANES), width)
    for start in range(0, columns, chunk):
        terms = jnp.dot(left, weight_ref[:, start : start + chunk], preferred_element_type=jnp.float32)
        for pair in range(0, chunk, 2 * LANES):
            found = jnp.zeros((8, LANES), jnp.float32)
            for d in range(4):
                turn = terms[8 * d : 8 * (d + 1), pair : pair + 2 * LANES]
                turn = jnp.where(subs < 4, turn[:, :LANES], turn[:, LANES:])
                turn = pltpu.roll(turn, d * width, 1) if d else turn
                found = jnp.where(block == (subs + d) % 4, turn, found)
            at = (start + pair) // width
            out_ref[at : at + 8, :] = found


def finish_kernel(terms_ref, part_ref, bound_ref, output_ref, attention_ref, mass_ref):
    batch, heads, pages = bound_ref.shape
    shards = part_ref.shape[0] // 2
    group = HQ // KVH
    groups = heads // group
    width = LANES // 4
    sums = jnp.sum(terms_ref[...], axis=0, keepdims=True)
    attention = merged_line(part_ref)
    for b in range(batch):
        columns = slice(b * width, (b + 1) * width)
        output_ref[b : b + 1, :] = sums[:, columns].astype(jnp.bfloat16)
        attention_ref[b : b + 1, :] = attention[:, columns]
    logs = part_ref[pl.ds(1, shards, stride=2), :]
    peak = jnp.max(logs, axis=0, keepdims=True)
    line = peak + jnp.log(jnp.sum(jnp.exp(logs - peak), axis=0, keepdims=True))
    lanes = lax.broadcasted_iota(jnp.int32, (group, LANES), 1)
    subs = lax.broadcasted_iota(jnp.int32, (group, LANES), 0)
    for b in range(batch):
        for g in range(groups):
            n = b * groups + g
            column = jnp.sum(
                jnp.where(lanes == subs * (batch * groups) + n, line, 0.0), axis=1, keepdims=True
            )
            rows = slice(g * group, (g + 1) * group)
            mass_ref[b, rows, :] = jnp.exp(bound_ref[b, rows, :] - column)


def call(kernel, out_shape, args, specs, nbytes, scratch=(), limit=32):
    many = isinstance(out_shape, tuple)
    return pl.pallas_call(
        kernel,
        out_shape=out_shape,
        in_specs=specs,
        out_specs=tuple(VMEM for _ in out_shape) if many else VMEM,
        scratch_shapes=list(scratch),
        compiler_params=pltpu.CompilerParams(vmem_limit_bytes=limit << 20),
        cost_estimate=pl.CostEstimate(flops=0, bytes_accessed=nbytes, transcendentals=0),
    )(*args)


def exchanged(x, axis):
    rows = lax.axis_size(axis)
    sent = x.reshape(rows, x.shape[0] // rows, x.shape[1])
    return lax.all_to_all(sent, axis, 0, 0, tiled=True).reshape(x.shape)


def local(queries, key_cache, value_cache, page_list, shard_counts, out_weight):
    batch, groups, tokens, dim = key_cache.shape
    pages = tokens // PAGE
    shards = lax.axis_size("seq")
    devices = lax.axis_size("head") * shards
    pairs = batch * groups
    heads = groups * (HQ // KVH)
    width = queries.shape[1]
    f32, bf16 = jnp.float32, jnp.bfloat16
    S = jax.ShapeDtypeStruct

    sent = call(
        functools.partial(spread_kernel, shards),
        S((shards, LANES), f32),
        (queries,),
        [VMEM],
        1 << 16,
    )
    sent, page_list, shard_counts = lax.optimization_barrier((sent, page_list, shard_counts))
    lists = jnp.concatenate([page_list, shard_counts], axis=2)
    live, starts, ends, keys = call(
        prepare_kernel,
        (
            S((pairs, LANES), f32),
            S((pairs, LANES), jnp.int32),
            S((pairs, pages, 2 * dim), bf16),
            S((pairs, CAP * PAGE, dim), bf16),
        ),
        (lists, key_cache),
        [VMEM, HBM],
        1 << 22,
        [
            pltpu.SMEM((pairs, LANES), jnp.int32),
            pltpu.VMEM((pairs, tokens, dim), bf16),
            pltpu.SemaphoreType.DMA,
            pltpu.SemaphoreType.DMA((pairs,)),
        ],
        52,
    )
    gathered = exchanged(sent, "seq")
    parts, bound = call(
        scores_kernel,
        (S((2 * shards, LANES), f32), S((batch, heads, pages), f32)),
        (live, starts, gathered, ends, keys, value_cache),
        [VMEM, VMEM, VMEM, VMEM, VMEM, VMEM],
        1 << 20,
        [pltpu.SMEM((pairs, LANES), jnp.int32), pltpu.SemaphoreType.DMA],
    )
    arrived = exchanged(parts, "seq")
    terms = call(project_kernel, S((devices, LANES), f32), (arrived, out_weight), [VMEM, VMEM], 1 << 20)
    landed = exchanged(terms, ("head", "seq"))
    return call(
        finish_kernel,
        (S((batch, width), bf16), S((batch, width), bf16), S((batch, heads, pages), f32)),
        (landed, arrived, bound),
        [VMEM, VMEM, VMEM],
        1 << 18,
    )


def solution(mesh):
    return jax.shard_map(
        local,
        mesh=mesh,
        in_specs=(
            P(None, ("head", "seq")),
            P(None, "head", "seq", None),
            P(None, "head", "seq", None),
            P(None, "head", None),
            P(None, "head", None),
            P(("head", "seq"), None),
        ),
        out_specs=(P(None, ("head", "seq")), P(None, ("head", "seq")), P(None, "head", "seq")),
        check_vma=False,
    )
```

```python
import functools
import math

import jax
import jax.numpy as jnp
from jax import lax
from jax.experimental import pallas as pl
from jax.experimental.pallas import tpu as pltpu
from jax.sharding import PartitionSpec as P

HQ = 64
KVH = 8
HD = 128
PAGE = 16
CAP = 8
SELECT = 256
LANES = 128
NEGATIVE = -1e30
SCALE = 1.0 / math.sqrt(HD)

VMEM = pl.BlockSpec(memory_space=pltpu.VMEM)
HBM = pl.BlockSpec(memory_space=pltpu.HBM)


def block_lanes(shape, width):
    return lax.broadcasted_iota(jnp.int32, shape, 1) // width


def spread_kernel(copies, query_ref, out_ref):
    rows = query_ref[...].astype(jnp.float32)
    line = jnp.concatenate([rows[b : b + 1, :] for b in range(rows.shape[0])], axis=1)
    out_ref[...] = jnp.broadcast_to(line, (copies, LANES))


def folded_rows(pieces, combine):
    rows = lax.broadcasted_iota(jnp.int32, pieces[0].shape, 0)

    def step(first, second, keep, shift):
        kept = jnp.where(keep, first, second)
        other = jnp.where(keep, second, first)
        return combine(kept, pltpu.roll(other, shift, 0))

    def four(a, b, c, d, turn):
        at = (rows + turn) % 8
        left = step(a, b, at < 4, 4)
        right = step(c, d, (at < 2) | (at >= 6), 4)
        return step(left, right, at % 4 >= 2, 2)

    odd = four(pieces[3], pieces[7], pieces[1], pieces[5], 0)
    even = four(pieces[2], pieces[6], pieces[0], pieces[4], 1)
    return step(odd, even, rows % 2 == 1, 1)


def prepare_kernel(
    lists_ref, key_hbm,
    live_ref, start_ref, ends_ref, keys_out,
    spot_ref, key_ref, spot_sem, key_sems,
):
    batch, groups, tokens, dim = key_hbm.shape
    pages = tokens // PAGE
    shard = lax.axis_index("seq")
    pairs = [(b, g) for b in range(batch) for g in range(groups)]
    key_copies = [
        pltpu.make_async_copy(key_hbm.at[b, g], key_ref.at[n], key_sems.at[n])
        for n, (b, g) in enumerate(pairs)
    ]
    for copy in key_copies:
        copy.start()
    lists = jnp.concatenate([lists_ref[b] for b in range(batch)], axis=0).astype(jnp.float32)
    listed, counts = lists[:, :SELECT], lists[:, SELECT:]
    index = lax.broadcasted_iota(jnp.int32, counts.shape, 1)
    offset = jnp.sum(jnp.where(index < shard, counts, 0.0), axis=1, keepdims=True).astype(jnp.int32)
    count = jnp.sum(jnp.where(index == shard, counts, 0.0), axis=1, keepdims=True).astype(jnp.int32)
    lanes = lax.broadcasted_iota(jnp.int32, (len(pairs), LANES), 1)
    live_ref[...] = jnp.where(lanes // PAGE < count, 1.0, 0.0)
    place = lax.broadcasted_iota(jnp.int32, listed.shape, 1)
    page = jnp.zeros((len(pairs), LANES), jnp.float32)
    for slot in range(CAP):
        found = jnp.sum(jnp.where(place == offset + slot, listed, 0.0), axis=1, keepdims=True)
        page = jnp.where(lanes == slot, found, page)
    start_ref[...] = jnp.clip(page.astype(jnp.int32) - shard * pages, 0, pages - 1) * PAGE
    spots = pltpu.make_async_copy(start_ref, spot_ref, spot_sem)
    spots.start()
    for n in range(len(pairs)):
        key_copies[n].wait()
        for first in range(0, pages, 16):
            largest, smallest = [], []
            for half in (first, first + 8):
                wide = key_ref[n, half * PAGE : (half + 8) * PAGE, :].astype(jnp.float32)
                parts = [wide[8 * k : 8 * (k + 1)] for k in range(PAGE)]
                above = [jnp.maximum(parts[2 * k], parts[2 * k + 1]) for k in range(8)]
                below = [jnp.minimum(parts[2 * k], parts[2 * k + 1]) for k in range(8)]
                largest.append(folded_rows(above, jnp.maximum))
                smallest.append(folded_rows(below, jnp.minimum))
            at = slice(first, first + 16)
            ends_ref[n, at, :dim] = jnp.concatenate(largest, axis=0).astype(jnp.bfloat16)
            ends_ref[n, at, dim:] = jnp.concatenate(smallest, axis=0).astype(jnp.bfloat16)
    spots.wait()
    starts = [
        [pl.multiple_of(spot_ref[n, slot], PAGE) for slot in range(CAP)] for n in range(len(pairs))
    ]
    for n in range(len(pairs)):
        for slot in range(CAP):
            rows = slice(slot * PAGE, (slot + 1) * PAGE)
            keys_out[n, rows, :] = key_ref[n, pl.ds(starts[n][slot], PAGE), :]


def scores_kernel(
    live_ref, start_ref, query_ref, ends_ref, keys_ref, value_ref,
    part_ref, bound_ref,
    spot_ref, spot_sem,
):
    spots = pltpu.make_async_copy(start_ref, spot_ref, spot_sem)
    spots.start()
    batch, heads, _ = bound_ref.shape
    groups = live_ref.shape[0] // batch
    group = heads // groups
    width = LANES // 4
    quarters = [query_ref[pl.ds(q, heads, stride=4), :] for q in range(4)]
    lane_block = block_lanes((heads, LANES), width)

    def rows_of(b):
        found = jnp.zeros((heads, LANES), jnp.float32)
        for q in range(4):
            shift = (q - b) * width % LANES
            moved = pltpu.roll(quarters[q], shift, 1) if shift else quarters[q]
            found = jnp.where(lane_block == q, moved, found)
        return found

    lanes = lax.broadcasted_iota(jnp.int32, (group, LANES), 1)
    subs = lax.broadcasted_iota(jnp.int32, (group, LANES), 0)
    page_row = jnp.zeros((group, LANES), jnp.float32)
    head_rows = [jnp.zeros((group, LANES), jnp.float32) for _ in range(groups)]
    shares = []
    contract = (((1,), (1,)), ((), ()))
    for b in range(batch):
        rows = rows_of(b)
        for g in range(groups):
            n = b * groups + g
            query = rows[g * group : (g + 1) * group]
            signed = jnp.concatenate([jnp.maximum(query, 0.0), jnp.minimum(query, 0.0)], axis=1)
            bound = SCALE * lax.dot_general(
                signed.astype(jnp.bfloat16), ends_ref[n], contract, preferred_element_type=jnp.float32
            )
            bound_ref[b, g * group : (g + 1) * group, :] = bound
            peak = jnp.max(bound, axis=1, keepdims=True)
            mass = jnp.sum(jnp.exp(bound - peak), axis=1, keepdims=True)
            page_row = jnp.where(lanes == subs * (batch * groups) + n, peak + jnp.log(mass), page_row)
            scores = SCALE * lax.dot_general(
                query.astype(jnp.bfloat16), keys_ref[n], contract, preferred_element_type=jnp.float32
            )
            live = live_ref[n : n + 1, :] > 0.0
            scores = jnp.where(live, scores, NEGATIVE)
            top = jnp.max(scores, axis=1, keepdims=True)
            weights = jnp.where(live, jnp.exp(scores - top), 0.0)
            total = jnp.maximum(jnp.sum(weights, axis=1, keepdims=True), 1e-30)
            shares.append((weights.astype(jnp.bfloat16), total))
            head_rows[g] = jnp.where(
                lanes == LANES // 2 + b, top + jnp.log(total), head_rows[g]
            )
    spots.wait()
    mixed = []
    for b in range(batch):
        parts = []
        for g in range(groups):
            n = b * groups + g
            weights, total = shares[n]
            values = jnp.concatenate(
                [
                    value_ref[b, g, pl.ds(pl.multiple_of(spot_ref[n, slot], PAGE), PAGE), :]
                    for slot in range(CAP)
                ],
                axis=0,
            )
            parts.append(jnp.dot(weights, values, preferred_element_type=jnp.float32) / total)
        mixed.append(jnp.concatenate(parts, axis=0))
    page_line = jnp.sum(page_row, axis=0, keepdims=True)
    seconds = jnp.concatenate(head_rows, axis=0) + page_line
    for q in range(4):
        line = jnp.zeros((heads, LANES), jnp.float32)
        for b in range(batch):
            shift = (b - q) * width % LANES
            moved = pltpu.roll(mixed[b], shift, 1) if shift else mixed[b]
            line = jnp.where(lane_block == b, moved, line)
        part_ref[pl.ds(2 * q, heads, stride=8), :] = line
        part_ref[pl.ds(2 * q + 1, heads, stride=8), :] = seconds


def project_kernel(part_ref, weight_ref, out_ref, line_ref):
    width = LANES // 4
    columns = weight_ref.shape[1]
    chunk = 4 * LANES
    shards = part_ref.shape[0] // 2
    values = part_ref[pl.ds(0, shards, stride=2), :]
    logs = part_ref[pl.ds(1, shards, stride=2), :]
    peak = jnp.max(logs, axis=0, keepdims=True)
    shares = jnp.exp(logs - peak)
    lane_block = block_lanes((shards, LANES), width)
    spread = jnp.zeros((shards, LANES), jnp.float32)
    for b in range(4):
        at = LANES // 2 + b
        spread = jnp.where(lane_block == b, shares[:, at : at + 1], spread)
    line = jnp.sum(spread * values, axis=0, keepdims=True) / jnp.sum(spread, axis=0, keepdims=True)
    line = line.astype(jnp.bfloat16).astype(jnp.float32)
    line_ref[0:1, :] = line
    line_ref[1:2, :] = peak + jnp.log(jnp.sum(shares, axis=0, keepdims=True))
    rows = [line[:, b * width : (b + 1) * width] for b in range(4)]
    small = lax.broadcasted_iota(jnp.int32, (8, width), 0)
    sides = []
    for d in range(4):
        side = jnp.zeros((8, width), jnp.float32)
        for b in range(4):
            side = jnp.where((small + d) % 4 == b, rows[b], side)
        sides.append(side)
    left = jnp.concatenate(sides, axis=0).astype(jnp.bfloat16)
    subs = lax.broadcasted_iota(jnp.int32, (8, LANES), 0)
    block = block_lanes((8, LANES), width)
    for start in range(0, columns, chunk):
        terms = jnp.dot(left, weight_ref[:, start : start + chunk], preferred_element_type=jnp.float32)
        for pair in range(0, chunk, 2 * LANES):
            found = jnp.zeros((8, LANES), jnp.float32)
            for d in range(4):
                turn = terms[8 * d : 8 * (d + 1), pair : pair + 2 * LANES]
                turn = jnp.where(subs < 4, turn[:, :LANES], turn[:, LANES:])
                turn = pltpu.roll(turn, d * width, 1) if d else turn
                found = jnp.where(block == (subs + d) % 4, turn, found)
            at = (start + pair) // width
            out_ref[at : at + 8, :] = found


def finish_kernel(terms_ref, line_ref, bound_ref, output_ref, attention_ref, mass_ref):
    batch, heads, pages = bound_ref.shape
    group = HQ // KVH
    groups = heads // group
    width = LANES // 4
    sums = jnp.sum(terms_ref[...], axis=0, keepdims=True)
    attention = line_ref[0:1, :].astype(jnp.bfloat16)
    for b in range(batch):
        columns = slice(b * width, (b + 1) * width)
        output_ref[b : b + 1, :] = sums[:, columns].astype(jnp.bfloat16)
        attention_ref[b : b + 1, :] = attention[:, columns]
    line = line_ref[1:2, :]
    lanes = lax.broadcasted_iota(jnp.int32, (group, LANES), 1)
    subs = lax.broadcasted_iota(jnp.int32, (group, LANES), 0)
    for b in range(batch):
        for g in range(groups):
            n = b * groups + g
            column = jnp.sum(
                jnp.where(lanes == subs * (batch * groups) + n, line, 0.0), axis=1, keepdims=True
            )
            rows = slice(g * group, (g + 1) * group)
            mass_ref[b, rows, :] = jnp.exp(bound_ref[b, rows, :] - column)


def call(kernel, out_shape, args, specs, nbytes, scratch=(), limit=32):
    many = isinstance(out_shape, tuple)
    return pl.pallas_call(
        kernel,
        out_shape=out_shape,
        in_specs=specs,
        out_specs=tuple(VMEM for _ in out_shape) if many else VMEM,
        scratch_shapes=list(scratch),
        compiler_params=pltpu.CompilerParams(vmem_limit_bytes=limit << 20),
        cost_estimate=pl.CostEstimate(flops=0, bytes_accessed=nbytes, transcendentals=0),
    )(*args)


def exchanged(x, axis):
    rows = lax.axis_size(axis)
    sent = x.reshape(rows, x.shape[0] // rows, x.shape[1])
    return lax.all_to_all(sent, axis, 0, 0, tiled=True).reshape(x.shape)


def local(queries, key_cache, value_cache, page_list, shard_counts, out_weight):
    batch, groups, tokens, dim = key_cache.shape
    pages = tokens // PAGE
    shards = lax.axis_size("seq")
    devices = lax.axis_size("head") * shards
    pairs = batch * groups
    heads = groups * (HQ // KVH)
    width = queries.shape[1]
    f32, bf16 = jnp.float32, jnp.bfloat16
    S = jax.ShapeDtypeStruct

    sent = call(
        functools.partial(spread_kernel, shards),
        S((shards, LANES), f32),
        (queries,),
        [VMEM],
        1 << 16,
    )
    sent, page_list, shard_counts = lax.optimization_barrier((sent, page_list, shard_counts))
    lists = jnp.concatenate([page_list, shard_counts], axis=2)
    live, starts, ends, keys = call(
        prepare_kernel,
        (
            S((pairs, LANES), f32),
            S((pairs, LANES), jnp.int32),
            S((pairs, pages, 2 * dim), bf16),
            S((pairs, CAP * PAGE, dim), bf16),
        ),
        (lists, key_cache),
        [VMEM, HBM],
        1 << 22,
        [
            pltpu.SMEM((pairs, LANES), jnp.int32),
            pltpu.VMEM((pairs, tokens, dim), bf16),
            pltpu.SemaphoreType.DMA,
            pltpu.SemaphoreType.DMA((pairs,)),
        ],
        52,
    )
    gathered = exchanged(sent, "seq")
    parts, bound = call(
        scores_kernel,
        (S((2 * shards, LANES), f32), S((batch, heads, pages), f32)),
        (live, starts, gathered, ends, keys, value_cache),
        [VMEM, VMEM, VMEM, VMEM, VMEM, VMEM],
        1 << 20,
        [pltpu.SMEM((pairs, LANES), jnp.int32), pltpu.SemaphoreType.DMA],
    )
    arrived = exchanged(parts, "seq")
    terms, line = call(
        project_kernel,
        (S((devices, LANES), f32), S((2, LANES), f32)),
        (arrived, out_weight),
        [VMEM, VMEM],
        1 << 20,
    )
    landed = exchanged(terms, ("head", "seq"))
    return call(
        finish_kernel,
        (S((batch, width), bf16), S((batch, width), bf16), S((batch, heads, pages), f32)),
        (landed, line, bound),
        [VMEM, VMEM, VMEM],
        1 << 18,
    )


def solution(mesh):
    return jax.shard_map(
        local,
        mesh=mesh,
        in_specs=(
            P(None, ("head", "seq")),
            P(None, "head", "seq", None),
            P(None, "head", "seq", None),
            P(None, "head", None),
            P(None, "head", None),
            P(("head", "seq"), None),
        ),
        out_specs=(P(None, ("head", "seq")), P(None, ("head", "seq")), P(None, "head", "seq")),
        check_vma=False,
    )
```

```python
import functools
import math

import jax
import jax.numpy as jnp
from jax import lax
from jax.experimental import pallas as pl
from jax.experimental.pallas import tpu as pltpu
from jax.sharding import PartitionSpec as P

HQ = 64
KVH = 8
HD = 128
PAGE = 16
CAP = 8
SELECT = 256
LANES = 128
NEGATIVE = -1e30
SCALE = 1.0 / math.sqrt(HD)

VMEM = pl.BlockSpec(memory_space=pltpu.VMEM)
HBM = pl.BlockSpec(memory_space=pltpu.HBM)


def block_lanes(shape, width):
    return lax.broadcasted_iota(jnp.int32, shape, 1) // width


def spread_kernel(copies, query_hbm, out_ref, query_ref, arrived):
    copy = pltpu.make_async_copy(query_hbm, query_ref, arrived)
    copy.start()
    copy.wait()
    rows = query_ref[...].astype(jnp.float32)
    line = jnp.concatenate([rows[b : b + 1, :] for b in range(rows.shape[0])], axis=1)
    out_ref[...] = jnp.broadcast_to(line, (copies, LANES))


def folded_rows(pieces, combine):
    rows = lax.broadcasted_iota(jnp.int32, pieces[0].shape, 0)

    def step(first, second, keep, shift):
        kept = jnp.where(keep, first, second)
        other = jnp.where(keep, second, first)
        return combine(kept, pltpu.roll(other, shift, 0))

    def four(a, b, c, d, turn):
        at = (rows + turn) % 8
        left = step(a, b, at < 4, 4)
        right = step(c, d, (at < 2) | (at >= 6), 4)
        return step(left, right, at % 4 >= 2, 2)

    odd = four(pieces[3], pieces[7], pieces[1], pieces[5], 0)
    even = four(pieces[2], pieces[6], pieces[0], pieces[4], 1)
    return step(odd, even, rows % 2 == 1, 1)


def prepare_kernel(
    lists_ref, key_hbm,
    live_ref, start_ref, ends_ref, keys_out,
    spot_ref, key_ref, spot_sem, key_sems,
):
    batch, groups, tokens, dim = key_hbm.shape
    pages = tokens // PAGE
    shard = lax.axis_index("seq")
    pairs = [(b, g) for b in range(batch) for g in range(groups)]
    key_copies = [
        pltpu.make_async_copy(key_hbm.at[b, g], key_ref.at[n], key_sems.at[n])
        for n, (b, g) in enumerate(pairs)
    ]
    for copy in key_copies:
        copy.start()
    lists = jnp.concatenate([lists_ref[b] for b in range(batch)], axis=0).astype(jnp.float32)
    listed, counts = lists[:, :SELECT], lists[:, SELECT:]
    index = lax.broadcasted_iota(jnp.int32, counts.shape, 1)
    offset = jnp.sum(jnp.where(index < shard, counts, 0.0), axis=1, keepdims=True).astype(jnp.int32)
    count = jnp.sum(jnp.where(index == shard, counts, 0.0), axis=1, keepdims=True).astype(jnp.int32)
    lanes = lax.broadcasted_iota(jnp.int32, (len(pairs), LANES), 1)
    live_ref[...] = jnp.where(lanes // PAGE < count, 1.0, 0.0)
    place = lax.broadcasted_iota(jnp.int32, listed.shape, 1)
    page = jnp.zeros((len(pairs), LANES), jnp.float32)
    for slot in range(CAP):
        found = jnp.sum(jnp.where(place == offset + slot, listed, 0.0), axis=1, keepdims=True)
        page = jnp.where(lanes == slot, found, page)
    start_ref[...] = jnp.clip(page.astype(jnp.int32) - shard * pages, 0, pages - 1) * PAGE
    spots = pltpu.make_async_copy(start_ref, spot_ref, spot_sem)
    spots.start()
    for n in range(len(pairs)):
        key_copies[n].wait()
        for first in range(0, pages, 16):
            largest, smallest = [], []
            for half in (first, first + 8):
                wide = key_ref[n, half * PAGE : (half + 8) * PAGE, :].astype(jnp.float32)
                parts = [wide[8 * k : 8 * (k + 1)] for k in range(PAGE)]
                above = [jnp.maximum(parts[2 * k], parts[2 * k + 1]) for k in range(8)]
                below = [jnp.minimum(parts[2 * k], parts[2 * k + 1]) for k in range(8)]
                largest.append(folded_rows(above, jnp.maximum))
                smallest.append(folded_rows(below, jnp.minimum))
            at = slice(first, first + 16)
            ends_ref[n, at, :dim] = jnp.concatenate(largest, axis=0).astype(jnp.bfloat16)
            ends_ref[n, at, dim:] = jnp.concatenate(smallest, axis=0).astype(jnp.bfloat16)
    spots.wait()
    starts = [
        [pl.multiple_of(spot_ref[n, slot], PAGE) for slot in range(CAP)] for n in range(len(pairs))
    ]
    for n in range(len(pairs)):
        for slot in range(CAP):
            rows = slice(slot * PAGE, (slot + 1) * PAGE)
            keys_out[n, rows, :] = key_ref[n, pl.ds(starts[n][slot], PAGE), :]


def scores_kernel(
    live_ref, start_ref, query_ref, ends_ref, keys_ref, value_ref,
    part_ref, bound_ref,
    spot_ref, spot_sem,
):
    spots = pltpu.make_async_copy(start_ref, spot_ref, spot_sem)
    spots.start()
    batch, heads, _ = bound_ref.shape
    groups = live_ref.shape[0] // batch
    group = heads // groups
    width = LANES // 4
    quarters = [query_ref[pl.ds(q, heads, stride=4), :] for q in range(4)]
    lane_block = block_lanes((heads, LANES), width)

    def rows_of(b):
        found = jnp.zeros((heads, LANES), jnp.float32)
        for q in range(4):
            shift = (q - b) * width % LANES
            moved = pltpu.roll(quarters[q], shift, 1) if shift else quarters[q]
            found = jnp.where(lane_block == q, moved, found)
        return found

    lanes = lax.broadcasted_iota(jnp.int32, (group, LANES), 1)
    subs = lax.broadcasted_iota(jnp.int32, (group, LANES), 0)
    page_row = jnp.zeros((group, LANES), jnp.float32)
    head_rows = [jnp.zeros((group, LANES), jnp.float32) for _ in range(groups)]
    shares = []
    contract = (((1,), (1,)), ((), ()))
    for b in range(batch):
        rows = rows_of(b)
        for g in range(groups):
            n = b * groups + g
            query = rows[g * group : (g + 1) * group]
            signed = jnp.concatenate([jnp.maximum(query, 0.0), jnp.minimum(query, 0.0)], axis=1)
            bound = SCALE * lax.dot_general(
                signed.astype(jnp.bfloat16), ends_ref[n], contract, preferred_element_type=jnp.float32
            )
            bound_ref[b, g * group : (g + 1) * group, :] = bound
            peak = jnp.max(bound, axis=1, keepdims=True)
            mass = jnp.sum(jnp.exp(bound - peak), axis=1, keepdims=True)
            page_row = jnp.where(lanes == subs * (batch * groups) + n, peak + jnp.log(mass), page_row)
            scores = SCALE * lax.dot_general(
                query.astype(jnp.bfloat16), keys_ref[n], contract, preferred_element_type=jnp.float32
            )
            live = live_ref[n : n + 1, :] > 0.0
            scores = jnp.where(live, scores, NEGATIVE)
            top = jnp.max(scores, axis=1, keepdims=True)
            weights = jnp.where(live, jnp.exp(scores - top), 0.0)
            total = jnp.maximum(jnp.sum(weights, axis=1, keepdims=True), 1e-30)
            shares.append((weights.astype(jnp.bfloat16), total))
            head_rows[g] = jnp.where(
                lanes == LANES // 2 + b, top + jnp.log(total), head_rows[g]
            )
    spots.wait()
    mixed = []
    for b in range(batch):
        parts = []
        for g in range(groups):
            n = b * groups + g
            weights, total = shares[n]
            values = jnp.concatenate(
                [
                    value_ref[b, g, pl.ds(pl.multiple_of(spot_ref[n, slot], PAGE), PAGE), :]
                    for slot in range(CAP)
                ],
                axis=0,
            )
            parts.append(jnp.dot(weights, values, preferred_element_type=jnp.float32) / total)
        mixed.append(jnp.concatenate(parts, axis=0))
    page_line = jnp.sum(page_row, axis=0, keepdims=True)
    seconds = jnp.concatenate(head_rows, axis=0) + page_line
    for q in range(4):
        line = jnp.zeros((heads, LANES), jnp.float32)
        for b in range(batch):
            shift = (b - q) * width % LANES
            moved = pltpu.roll(mixed[b], shift, 1) if shift else mixed[b]
            line = jnp.where(lane_block == b, moved, line)
        part_ref[pl.ds(2 * q, heads, stride=8), :] = line
        part_ref[pl.ds(2 * q + 1, heads, stride=8), :] = seconds


def project_kernel(part_ref, weight_ref, out_ref, line_ref):
    width = LANES // 4
    columns = weight_ref.shape[1]
    chunk = 4 * LANES
    shards = part_ref.shape[0] // 2
    values = part_ref[pl.ds(0, shards, stride=2), :]
    logs = part_ref[pl.ds(1, shards, stride=2), :]
    peak = jnp.max(logs, axis=0, keepdims=True)
    shares = jnp.exp(logs - peak)
    lane_block = block_lanes((shards, LANES), width)
    spread = jnp.zeros((shards, LANES), jnp.float32)
    for b in range(4):
        at = LANES // 2 + b
        spread = jnp.where(lane_block == b, shares[:, at : at + 1], spread)
    line = jnp.sum(spread * values, axis=0, keepdims=True) / jnp.sum(spread, axis=0, keepdims=True)
    line = line.astype(jnp.bfloat16).astype(jnp.float32)
    line_ref[0:1, :] = line
    line_ref[1:2, :] = peak + jnp.log(jnp.sum(shares, axis=0, keepdims=True))
    rows = [line[:, b * width : (b + 1) * width] for b in range(4)]
    small = lax.broadcasted_iota(jnp.int32, (8, width), 0)
    sides = []
    for d in range(4):
        side = jnp.zeros((8, width), jnp.float32)
        for b in range(4):
            side = jnp.where((small + d) % 4 == b, rows[b], side)
        sides.append(side)
    left = jnp.concatenate(sides, axis=0).astype(jnp.bfloat16)
    subs = lax.broadcasted_iota(jnp.int32, (8, LANES), 0)
    block = block_lanes((8, LANES), width)
    for start in range(0, columns, chunk):
        terms = jnp.dot(left, weight_ref[:, start : start + chunk], preferred_element_type=jnp.float32)
        for pair in range(0, chunk, 2 * LANES):
            found = jnp.zeros((8, LANES), jnp.float32)
            for d in range(4):
                turn = terms[8 * d : 8 * (d + 1), pair : pair + 2 * LANES]
                turn = jnp.where(subs < 4, turn[:, :LANES], turn[:, LANES:])
                turn = pltpu.roll(turn, d * width, 1) if d else turn
                found = jnp.where(block == (subs + d) % 4, turn, found)
            at = (start + pair) // width
            out_ref[at : at + 8, :] = found


def finish_kernel(terms_ref, line_ref, bound_ref, output_ref, attention_ref, mass_ref):
    batch, heads, pages = bound_ref.shape
    group = HQ // KVH
    groups = heads // group
    width = LANES // 4
    sums = jnp.sum(terms_ref[...], axis=0, keepdims=True)
    attention = line_ref[0:1, :].astype(jnp.bfloat16)
    for b in range(batch):
        columns = slice(b * width, (b + 1) * width)
        output_ref[b : b + 1, :] = sums[:, columns].astype(jnp.bfloat16)
        attention_ref[b : b + 1, :] = attention[:, columns]
    line = line_ref[1:2, :]
    lanes = lax.broadcasted_iota(jnp.int32, (group, LANES), 1)
    subs = lax.broadcasted_iota(jnp.int32, (group, LANES), 0)
    for b in range(batch):
        for g in range(groups):
            n = b * groups + g
            column = jnp.sum(
                jnp.where(lanes == subs * (batch * groups) + n, line, 0.0), axis=1, keepdims=True
            )
            rows = slice(g * group, (g + 1) * group)
            mass_ref[b, rows, :] = jnp.exp(bound_ref[b, rows, :] - column)


def call(kernel, out_shape, args, specs, nbytes, scratch=(), limit=32):
    many = isinstance(out_shape, tuple)
    return pl.pallas_call(
        kernel,
        out_shape=out_shape,
        in_specs=specs,
        out_specs=tuple(VMEM for _ in out_shape) if many else VMEM,
        scratch_shapes=list(scratch),
        compiler_params=pltpu.CompilerParams(vmem_limit_bytes=limit << 20),
        cost_estimate=pl.CostEstimate(flops=0, bytes_accessed=nbytes, transcendentals=0),
    )(*args)


def exchanged(x, axis):
    rows = lax.axis_size(axis)
    sent = x.reshape(rows, x.shape[0] // rows, x.shape[1])
    return lax.all_to_all(sent, axis, 0, 0, tiled=True).reshape(x.shape)


def local(queries, key_cache, value_cache, page_list, shard_counts, out_weight):
    batch, groups, tokens, dim = key_cache.shape
    pages = tokens // PAGE
    shards = lax.axis_size("seq")
    devices = lax.axis_size("head") * shards
    pairs = batch * groups
    heads = groups * (HQ // KVH)
    width = queries.shape[1]
    f32, bf16 = jnp.float32, jnp.bfloat16
    S = jax.ShapeDtypeStruct

    sent = call(
        functools.partial(spread_kernel, shards),
        S((shards, LANES), f32),
        (queries,),
        [HBM],
        1 << 16,
        [pltpu.VMEM(queries.shape, bf16), pltpu.SemaphoreType.DMA],
        62,
    )
    sent, page_list, shard_counts = lax.optimization_barrier((sent, page_list, shard_counts))
    lists = jnp.concatenate([page_list, shard_counts], axis=2)
    live, starts, ends, keys = call(
        prepare_kernel,
        (
            S((pairs, LANES), f32),
            S((pairs, LANES), jnp.int32),
            S((pairs, pages, 2 * dim), bf16),
            S((pairs, CAP * PAGE, dim), bf16),
        ),
        (lists, key_cache),
        [VMEM, HBM],
        1 << 22,
        [
            pltpu.SMEM((pairs, LANES), jnp.int32),
            pltpu.VMEM((pairs, tokens, dim), bf16),
            pltpu.SemaphoreType.DMA,
            pltpu.SemaphoreType.DMA((pairs,)),
        ],
        52,
    )
    gathered = exchanged(sent, "seq")
    parts, bound = call(
        scores_kernel,
        (S((2 * shards, LANES), f32), S((batch, heads, pages), f32)),
        (live, starts, gathered, ends, keys, value_cache),
        [VMEM, VMEM, VMEM, VMEM, VMEM, VMEM],
        1 << 20,
        [pltpu.SMEM((pairs, LANES), jnp.int32), pltpu.SemaphoreType.DMA],
    )
    arrived = exchanged(parts, "seq")
    terms, line = call(
        project_kernel,
        (S((devices, LANES), f32), S((2, LANES), f32)),
        (arrived, out_weight),
        [VMEM, VMEM],
        1 << 20,
    )
    landed = exchanged(terms, ("head", "seq"))
    return call(
        finish_kernel,
        (S((batch, width), bf16), S((batch, width), bf16), S((batch, heads, pages), f32)),
        (landed, line, bound),
        [VMEM, VMEM, VMEM],
        1 << 18,
    )


def solution(mesh):
    return jax.shard_map(
        local,
        mesh=mesh,
        in_specs=(
            P(None, ("head", "seq")),
            P(None, "head", "seq", None),
            P(None, "head", "seq", None),
            P(None, "head", None),
            P(None, "head", None),
            P(("head", "seq"), None),
        ),
        out_specs=(P(None, ("head", "seq")), P(None, ("head", "seq")), P(None, "head", "seq")),
        check_vma=False,
    )
```

```python
import functools
import math

import jax
import jax.numpy as jnp
from jax import lax
from jax.experimental import pallas as pl
from jax.experimental.pallas import tpu as pltpu
from jax.sharding import PartitionSpec as P

HQ = 64
KVH = 8
HD = 128
PAGE = 16
CAP = 8
SELECT = 256
LANES = 128
NEGATIVE = -1e30
SCALE = 1.0 / math.sqrt(HD)

VMEM = pl.BlockSpec(memory_space=pltpu.VMEM)
HBM = pl.BlockSpec(memory_space=pltpu.HBM)


def block_lanes(shape, width):
    return lax.broadcasted_iota(jnp.int32, shape, 1) // width


def spread_kernel(copies, query_hbm, out_ref, query_ref, arrived):
    copy = pltpu.make_async_copy(query_hbm, query_ref, arrived)
    copy.start()
    copy.wait()
    rows = query_ref[...].astype(jnp.float32)
    line = jnp.concatenate([rows[b : b + 1, :] for b in range(rows.shape[0])], axis=1)
    out_ref[...] = jnp.broadcast_to(line, (copies, LANES))


def folded_rows(pieces, combine):
    rows = lax.broadcasted_iota(jnp.int32, pieces[0].shape, 0)

    def step(first, second, keep, shift):
        kept = jnp.where(keep, first, second)
        other = jnp.where(keep, second, first)
        return combine(kept, pltpu.roll(other, shift, 0))

    def four(a, b, c, d, turn):
        at = (rows + turn) % 8
        left = step(a, b, at < 4, 4)
        right = step(c, d, (at < 2) | (at >= 6), 4)
        return step(left, right, at % 4 >= 2, 2)

    odd = four(pieces[3], pieces[7], pieces[1], pieces[5], 0)
    even = four(pieces[2], pieces[6], pieces[0], pieces[4], 1)
    return step(odd, even, rows % 2 == 1, 1)


def prepare_kernel(
    lists_ref, key_hbm,
    live_ref, start_ref, ends_ref, keys_out,
    spot_ref, key_ref, spot_sem, key_sems,
):
    batch, groups, tokens, dim = key_hbm.shape
    pages = tokens // PAGE
    shard = lax.axis_index("seq")
    pairs = [(b, g) for b in range(batch) for g in range(groups)]
    key_copies = [
        pltpu.make_async_copy(key_hbm.at[b, g], key_ref.at[n], key_sems.at[n])
        for n, (b, g) in enumerate(pairs)
    ]
    for copy in key_copies:
        copy.start()
    lists = jnp.concatenate([lists_ref[b] for b in range(batch)], axis=0).astype(jnp.float32)
    listed, counts = lists[:, :SELECT], lists[:, SELECT:]
    index = lax.broadcasted_iota(jnp.int32, counts.shape, 1)
    offset = jnp.sum(jnp.where(index < shard, counts, 0.0), axis=1, keepdims=True).astype(jnp.int32)
    count = jnp.sum(jnp.where(index == shard, counts, 0.0), axis=1, keepdims=True).astype(jnp.int32)
    lanes = lax.broadcasted_iota(jnp.int32, (len(pairs), LANES), 1)
    live_ref[...] = jnp.where(lanes // PAGE < count, 1.0, 0.0)
    place = lax.broadcasted_iota(jnp.int32, listed.shape, 1)
    page = jnp.zeros((len(pairs), LANES), jnp.float32)
    for slot in range(CAP):
        found = jnp.sum(jnp.where(place == offset + slot, listed, 0.0), axis=1, keepdims=True)
        page = jnp.where(lanes == slot, found, page)
    start_ref[...] = jnp.clip(page.astype(jnp.int32) - shard * pages, 0, pages - 1) * PAGE
    spots = pltpu.make_async_copy(start_ref, spot_ref, spot_sem)
    spots.start()
    spots.wait()
    starts = [
        [pl.multiple_of(spot_ref[n, slot], PAGE) for slot in range(CAP)] for n in range(len(pairs))
    ]
    for n in range(len(pairs)):
        key_copies[n].wait()
        for first in range(0, pages, 16):
            largest, smallest = [], []
            for half in (first, first + 8):
                wide = key_ref[n, half * PAGE : (half + 8) * PAGE, :].astype(jnp.float32)
                parts = [wide[8 * k : 8 * (k + 1)] for k in range(PAGE)]
                above = [jnp.maximum(parts[2 * k], parts[2 * k + 1]) for k in range(8)]
                below = [jnp.minimum(parts[2 * k], parts[2 * k + 1]) for k in range(8)]
                largest.append(folded_rows(above, jnp.maximum))
                smallest.append(folded_rows(below, jnp.minimum))
            at = slice(first, first + 16)
            ends_ref[n, at, :dim] = jnp.concatenate(largest, axis=0).astype(jnp.bfloat16)
            ends_ref[n, at, dim:] = jnp.concatenate(smallest, axis=0).astype(jnp.bfloat16)
        for slot in range(CAP):
            rows = slice(slot * PAGE, (slot + 1) * PAGE)
            keys_out[n, rows, :] = key_ref[n, pl.ds(starts[n][slot], PAGE), :]


def scores_kernel(
    live_ref, start_ref, query_ref, ends_ref, keys_ref, value_ref,
    part_ref, bound_ref,
    spot_ref, spot_sem,
):
    spots = pltpu.make_async_copy(start_ref, spot_ref, spot_sem)
    spots.start()
    batch, heads, _ = bound_ref.shape
    groups = live_ref.shape[0] // batch
    group = heads // groups
    width = LANES // 4
    quarters = [query_ref[pl.ds(q, heads, stride=4), :] for q in range(4)]
    lane_block = block_lanes((heads, LANES), width)

    def rows_of(b):
        found = jnp.zeros((heads, LANES), jnp.float32)
        for q in range(4):
            shift = (q - b) * width % LANES
            moved = pltpu.roll(quarters[q], shift, 1) if shift else quarters[q]
            found = jnp.where(lane_block == q, moved, found)
        return found

    lanes = lax.broadcasted_iota(jnp.int32, (group, LANES), 1)
    subs = lax.broadcasted_iota(jnp.int32, (group, LANES), 0)
    page_row = jnp.zeros((group, LANES), jnp.float32)
    head_rows = [jnp.zeros((group, LANES), jnp.float32) for _ in range(groups)]
    shares = []
    contract = (((1,), (1,)), ((), ()))
    for b in range(batch):
        rows = rows_of(b)
        for g in range(groups):
            n = b * groups + g
            query = rows[g * group : (g + 1) * group]
            signed = jnp.concatenate([jnp.maximum(query, 0.0), jnp.minimum(query, 0.0)], axis=1)
            bound = SCALE * lax.dot_general(
                signed.astype(jnp.bfloat16), ends_ref[n], contract, preferred_element_type=jnp.float32
            )
            bound_ref[b, g * group : (g + 1) * group, :] = bound
            peak = jnp.max(bound, axis=1, keepdims=True)
            mass = jnp.sum(jnp.exp(bound - peak), axis=1, keepdims=True)
            page_row = jnp.where(lanes == subs * (batch * groups) + n, peak + jnp.log(mass), page_row)
            scores = SCALE * lax.dot_general(
                query.astype(jnp.bfloat16), keys_ref[n], contract, preferred_element_type=jnp.float32
            )
            live = live_ref[n : n + 1, :] > 0.0
            scores = jnp.where(live, scores, NEGATIVE)
            top = jnp.max(scores, axis=1, keepdims=True)
            weights = jnp.where(live, jnp.exp(scores - top), 0.0)
            total = jnp.maximum(jnp.sum(weights, axis=1, keepdims=True), 1e-30)
            shares.append((weights.astype(jnp.bfloat16), total))
            head_rows[g] = jnp.where(
                lanes == LANES // 2 + b, top + jnp.log(total), head_rows[g]
            )
    spots.wait()
    mixed = []
    for b in range(batch):
        parts = []
        for g in range(groups):
            n = b * groups + g
            weights, total = shares[n]
            values = jnp.concatenate(
                [
                    value_ref[b, g, pl.ds(pl.multiple_of(spot_ref[n, slot], PAGE), PAGE), :]
                    for slot in range(CAP)
                ],
                axis=0,
            )
            parts.append(jnp.dot(weights, values, preferred_element_type=jnp.float32) / total)
        mixed.append(jnp.concatenate(parts, axis=0))
    page_line = jnp.sum(page_row, axis=0, keepdims=True)
    seconds = jnp.concatenate(head_rows, axis=0) + page_line
    for q in range(4):
        line = jnp.zeros((heads, LANES), jnp.float32)
        for b in range(batch):
            shift = (b - q) * width % LANES
            moved = pltpu.roll(mixed[b], shift, 1) if shift else mixed[b]
            line = jnp.where(lane_block == b, moved, line)
        part_ref[pl.ds(2 * q, heads, stride=8), :] = line
        part_ref[pl.ds(2 * q + 1, heads, stride=8), :] = seconds


def project_kernel(part_ref, weight_ref, out_ref, line_ref):
    width = LANES // 4
    columns = weight_ref.shape[1]
    chunk = 4 * LANES
    shards = part_ref.shape[0] // 2
    values = part_ref[pl.ds(0, shards, stride=2), :]
    logs = part_ref[pl.ds(1, shards, stride=2), :]
    peak = jnp.max(logs, axis=0, keepdims=True)
    shares = jnp.exp(logs - peak)
    lane_block = block_lanes((shards, LANES), width)
    spread = jnp.zeros((shards, LANES), jnp.float32)
    for b in range(4):
        at = LANES // 2 + b
        spread = jnp.where(lane_block == b, shares[:, at : at + 1], spread)
    line = jnp.sum(spread * values, axis=0, keepdims=True) / jnp.sum(spread, axis=0, keepdims=True)
    line = line.astype(jnp.bfloat16).astype(jnp.float32)
    line_ref[0:1, :] = line
    line_ref[1:2, :] = peak + jnp.log(jnp.sum(shares, axis=0, keepdims=True))
    rows = [line[:, b * width : (b + 1) * width] for b in range(4)]
    small = lax.broadcasted_iota(jnp.int32, (8, width), 0)
    sides = []
    for d in range(4):
        side = jnp.zeros((8, width), jnp.float32)
        for b in range(4):
            side = jnp.where((small + d) % 4 == b, rows[b], side)
        sides.append(side)
    left = jnp.concatenate(sides, axis=0).astype(jnp.bfloat16)
    subs = lax.broadcasted_iota(jnp.int32, (8, LANES), 0)
    block = block_lanes((8, LANES), width)
    for start in range(0, columns, chunk):
        terms = jnp.dot(left, weight_ref[:, start : start + chunk], preferred_element_type=jnp.float32)
        for pair in range(0, chunk, 2 * LANES):
            found = jnp.zeros((8, LANES), jnp.float32)
            for d in range(4):
                turn = terms[8 * d : 8 * (d + 1), pair : pair + 2 * LANES]
                turn = jnp.where(subs < 4, turn[:, :LANES], turn[:, LANES:])
                turn = pltpu.roll(turn, d * width, 1) if d else turn
                found = jnp.where(block == (subs + d) % 4, turn, found)
            at = (start + pair) // width
            out_ref[at : at + 8, :] = found


def finish_kernel(terms_ref, line_ref, bound_ref, output_ref, attention_ref, mass_ref):
    batch, heads, pages = bound_ref.shape
    group = HQ // KVH
    groups = heads // group
    width = LANES // 4
    sums = jnp.sum(terms_ref[...], axis=0, keepdims=True)
    attention = line_ref[0:1, :].astype(jnp.bfloat16)
    for b in range(batch):
        columns = slice(b * width, (b + 1) * width)
        output_ref[b : b + 1, :] = sums[:, columns].astype(jnp.bfloat16)
        attention_ref[b : b + 1, :] = attention[:, columns]
    line = line_ref[1:2, :]
    lanes = lax.broadcasted_iota(jnp.int32, (group, LANES), 1)
    subs = lax.broadcasted_iota(jnp.int32, (group, LANES), 0)
    for b in range(batch):
        for g in range(groups):
            n = b * groups + g
            column = jnp.sum(
                jnp.where(lanes == subs * (batch * groups) + n, line, 0.0), axis=1, keepdims=True
            )
            rows = slice(g * group, (g + 1) * group)
            mass_ref[b, rows, :] = jnp.exp(bound_ref[b, rows, :] - column)


def call(kernel, out_shape, args, specs, nbytes, scratch=(), limit=32):
    many = isinstance(out_shape, tuple)
    return pl.pallas_call(
        kernel,
        out_shape=out_shape,
        in_specs=specs,
        out_specs=tuple(VMEM for _ in out_shape) if many else VMEM,
        scratch_shapes=list(scratch),
        compiler_params=pltpu.CompilerParams(vmem_limit_bytes=limit << 20),
        cost_estimate=pl.CostEstimate(flops=0, bytes_accessed=nbytes, transcendentals=0),
    )(*args)


def exchanged(x, axis):
    rows = lax.axis_size(axis)
    sent = x.reshape(rows, x.shape[0] // rows, x.shape[1])
    return lax.all_to_all(sent, axis, 0, 0, tiled=True).reshape(x.shape)


def local(queries, key_cache, value_cache, page_list, shard_counts, out_weight):
    batch, groups, tokens, dim = key_cache.shape
    pages = tokens // PAGE
    shards = lax.axis_size("seq")
    devices = lax.axis_size("head") * shards
    pairs = batch * groups
    heads = groups * (HQ // KVH)
    width = queries.shape[1]
    f32, bf16 = jnp.float32, jnp.bfloat16
    S = jax.ShapeDtypeStruct

    sent = call(
        functools.partial(spread_kernel, shards),
        S((shards, LANES), f32),
        (queries,),
        [HBM],
        1 << 16,
        [pltpu.VMEM(queries.shape, bf16), pltpu.SemaphoreType.DMA],
        62,
    )
    sent, page_list, shard_counts = lax.optimization_barrier((sent, page_list, shard_counts))
    lists = jnp.concatenate([page_list, shard_counts], axis=2)
    live, starts, ends, keys = call(
        prepare_kernel,
        (
            S((pairs, LANES), f32),
            S((pairs, LANES), jnp.int32),
            S((pairs, pages, 2 * dim), bf16),
            S((pairs, CAP * PAGE, dim), bf16),
        ),
        (lists, key_cache),
        [VMEM, HBM],
        1 << 22,
        [
            pltpu.SMEM((pairs, LANES), jnp.int32),
            pltpu.VMEM((pairs, tokens, dim), bf16),
            pltpu.SemaphoreType.DMA,
            pltpu.SemaphoreType.DMA((pairs,)),
        ],
        52,
    )
    gathered = exchanged(sent, "seq")
    parts, bound = call(
        scores_kernel,
        (S((2 * shards, LANES), f32), S((batch, heads, pages), f32)),
        (live, starts, gathered, ends, keys, value_cache),
        [VMEM, VMEM, VMEM, VMEM, VMEM, VMEM],
        1 << 20,
        [pltpu.SMEM((pairs, LANES), jnp.int32), pltpu.SemaphoreType.DMA],
    )
    arrived = exchanged(parts, "seq")
    terms, line = call(
        project_kernel,
        (S((devices, LANES), f32), S((2, LANES), f32)),
        (arrived, out_weight),
        [VMEM, VMEM],
        1 << 20,
    )
    landed = exchanged(terms, ("head", "seq"))
    return call(
        finish_kernel,
        (S((batch, width), bf16), S((batch, width), bf16), S((batch, heads, pages), f32)),
        (landed, line, bound),
        [VMEM, VMEM, VMEM],
        1 << 18,
    )


def solution(mesh):
    return jax.shard_map(
        local,
        mesh=mesh,
        in_specs=(
            P(None, ("head", "seq")),
            P(None, "head", "seq", None),
            P(None, "head", "seq", None),
            P(None, "head", None),
            P(None, "head", None),
            P(("head", "seq"), None),
        ),
        out_specs=(P(None, ("head", "seq")), P(None, ("head", "seq")), P(None, "head", "seq")),
        check_vma=False,
    )
```
